256 devices in a mesh: dp: 32 (over z, x_hi, core), tensor: 8 (over y, x_lo).
Axes of the slice: x: 4 (x_hi: 2, x_lo: 2; x = x_hi * 2 + x_lo), y: 4, z: 8, core: 2. Of those that a mesh axis runs over, the one named last changes fastest.
Arguments:
- queries: bfloat16 [32768, 4096], P(('dp', 'tensor')), parts along dimension 0, may hold values from -120 to 120
- keys: bfloat16 [32768, 4096], P(('dp', 'tensor')), parts along dimension 0, may hold values from -8 to 8
- values: bfloat16 [32768, 4096], P(('dp', 'tensor')), parts along dimension 0, may hold values from -30 to 30
- segment_ids: int32 [32768], P('dp'), parts along dimension 0, may hold values from 0 to 3, never falling along the last dimension, each value on 1 to 512 neighbouring positions
- residual: bfloat16 [32768, 4096], P(('dp', 'tensor')), parts along dimension 0, may hold values from -6 to 6
- sub_gain: float32 [4096], P('tensor'), may hold values from 0.25 to 1.75
- sub_bias: float32 [4096], P('tensor'), may hold values from -3 to 3
- out_weight: bfloat16 [4096, 4096], P('tensor'), may hold values from -0.09375 to 0.09375
- post_gain: float32 [4096], replicated, may hold values from 0.25 to 1.75
- post_bias: float32 [4096], replicated, may hold values from -3 to 3
Outputs:
- block_out: bfloat16 [32768, 4096], P(('dp', 'tensor')), parts along dimension 0
The draws below stay inside these ranges and needn't reach their ends.
There are 32 independent parts, one for each index of `dp`. The reference program is written for one: setup_inputs(seed, part) draws one part's arguments, and reference() takes and returns one part's arrays. A program takes and returns all parts, laid end to end along the dimension named above; an argument that names none is the same for every part. Nothing has to cross between parts.
Inputs may be any that keep to these rules, and one draw needn't show every extreme that they name: `segment_ids`: document numbers never fall along the stretch; every number appears; a document spans at most 512 tokens, and one exactly that many.
All inputs are finite; a program needn't handle non-finite values.
Results may differ from the reference program's by a relative error of at most 0.0065.
Values may be sent and summed in bfloat16 or wider, within the bound.
A program may use at most 128 MiB of HBM per device.

```python
import math
import jax
import jax.numpy as jnp
import numpy as np
from jax import lax

D = 4096
HEADS = 32
HEAD_DIM = 128
DOCS = 4
TOK_DEV = 128
TOKENS = 1024
INNER = 4096
N_TENSOR = 8


def base_keys(key):
    return jnp.clip(jax.random.normal(key, (TOKENS, HEADS * HEAD_DIM), jnp.float32), -5.0, 5.0)


def draw_keys(key, part):
    drawn = base_keys(key)
    return drawn.astype(jnp.bfloat16)


def draw_queries(key, part):
    drawn = base_keys(key)
    key = jax.random.fold_in(key, 3)
    fresh = jnp.clip(jax.random.normal(key, drawn.shape, jnp.float32), -5.0, 5.0)
    return fresh.astype(jnp.bfloat16)


def draw_values(key, part):
    key = jax.random.fold_in(key, 7)
    sample_key = jax.random.fold_in(key, 11)
    shared_key = jax.random.fold_in(key, 13)
    feature_key = jax.random.fold_in(key, 17)
    width = HEADS * HEAD_DIM
    span = max(TOK_DEV // 2, 1)
    groups = (TOKENS + span - 1) // span
    block = (jnp.arange(TOKENS) // span).astype(jnp.int32)
    shared = jax.random.uniform(shared_key, (groups,), jnp.float32, -6.0, 6.0)
    per_feature = jax.random.uniform(feature_key, (groups, width), jnp.float32, -6.0, 6.0)
    offset = shared[block][:, None] + per_feature[block]
    head = (jnp.arange(width) // HEAD_DIM).astype(jnp.float32)
    growth = 3.0 ** (head / max(HEADS - 1, 1))
    sample = jnp.clip(jax.random.normal(sample_key, (TOKENS, width), jnp.float32), -5.0, 5.0)
    return jnp.clip(0.6 * sample * growth + growth + offset, -30.0, 30.0).astype(jnp.bfloat16)


def block_levels(key, dims, shards, least, high):
    def one(dim, shards_of):
        draws = jax.random.uniform(jax.random.fold_in(jax.random.fold_in(key, 6), dim), (shards_of,), jnp.float32, least / len(shards), high / len(shards))
        return jnp.repeat(jnp.exp(draws), dims[dim] // shards_of).reshape((-1,) + (1,) * (len(dims) - dim - 1))

    factor_of = one(*shards[0])
    for cut in shards[1:]:
        factor_of = factor_of * one(*cut)
    return factor_of


def profile(amount, total, limit, skew):
    weights = [(1 << 20) // math.isqrt(rank ** skew) + 1 for rank in range(2, amount + 1)]
    rest, given = total - limit - (amount - 1), [1] * (amount - 1)
    while rest > 0:
        free = [i for i in range(amount - 1) if given[i] < limit]
        mass, budget = sum([weights[i] for i in free]), rest
        for i in free:
            more = min(limit - given[i], max(1, budget * weights[i] // mass), rest)
            given[i] = given[i] + more
            rest = rest - more
    return np.array([limit] + given)


def ragged_sizes(own_key, number_of, total, reach, lean):
    if number_of == 2:
        one = jax.random.randint(own_key, (), max(1, total - reach), min(reach, total - 1) + 1)
        return jnp.stack([one, total - one])
    lengths = jnp.asarray(profile(number_of, total, reach, lean), jnp.int32)
    pairs = (number_of - 1) // 2
    source_of, sink = lengths[1:1 + 2 * pairs:2], lengths[2:2 + 2 * pairs:2]
    room = jnp.minimum(source_of - 1, reach - sink)
    shifted = jax.random.randint(jax.random.fold_in(own_key, 1), (pairs,), 0, 1 << 20) % (room + 1)
    lengths = lengths.at[1:1 + 2 * pairs:2].set(source_of - shifted).at[2:2 + 2 * pairs:2].set(sink + shifted)
    return lengths[jax.random.permutation(jax.random.fold_in(own_key, 2), number_of)]


def normal_values(key, shape, scale, most, split=(), held_as=jnp.bfloat16):
    result = jax.random.normal(key, shape, jnp.float32) * scale
    if len(split) > 0:
        result = block_levels(key, shape, split, -0.22, 0.18) * result
    return jnp.clip(result, min=-most, max=most).astype(held_as)


def setup_inputs(seed: int = 0, part: int = 0) -> dict:
    arg_keys = jax.random.split(jax.random.key(seed), 11)
    part_keys = jax.random.split(jax.random.fold_in(arg_keys[10], part), 11)
    queries = draw_queries(jax.random.fold_in(jax.random.fold_in(arg_keys[10], part), 71), part)
    keys = draw_keys(jax.random.fold_in(jax.random.fold_in(arg_keys[10], part), 71), part)
    values = draw_values(jax.random.fold_in(jax.random.fold_in(arg_keys[10], part), 71), part)
    segment_ids = jnp.searchsorted(jnp.cumsum(ragged_sizes(part_keys[3], DOCS, TOKENS, TOKENS // 2, 1)), jnp.arange(TOKENS), side="right").astype(jnp.int32)
    residual = normal_values(part_keys[4], (TOKENS, D), 1.0, 6.0, ((0, 8),))
    sub_gain = jnp.clip(1.0 + 0.15 * jax.random.normal(arg_keys[5], (INNER,), jnp.float32), 0.25, 1.75)
    sub_bias = normal_values(arg_keys[6], (INNER,), 0.5, 3.0, ((0, 8),), jnp.float32)
    out_weight = normal_values(arg_keys[7], (INNER, D), INNER ** -0.5, 0.09375, ((0, 8),))
    post_gain = jnp.clip(1.0 + 0.15 * jax.random.normal(arg_keys[8], (D,), jnp.float32), 0.25, 1.75)
    post_bias = normal_values(arg_keys[9], (D,), 0.5, 3.0, (), jnp.float32)
    return {"queries": queries, "keys": keys, "values": values, "segment_ids": segment_ids, "residual": residual, "sub_gain": sub_gain, "sub_bias": sub_bias, "out_weight": out_weight, "post_gain": post_gain, "post_bias": post_bias}


deep_alpha = 160.0 ** 0.25

def reference(queries, keys, values, segment_ids, residual, sub_gain, sub_bias, out_weight, post_gain, post_bias):
    count = queries.shape[0]
    q_all = queries.reshape(count, HEADS, HEAD_DIM).transpose(1, 0, 2)
    k_all = keys.reshape(count, HEADS, HEAD_DIM).transpose(1, 0, 2)
    v_all = values.reshape(count, HEADS, HEAD_DIM).transpose(1, 0, 2)
    position = jnp.arange(count)
    allowed = (segment_ids[:, None] == segment_ids[None, :]) & (position[None, :] <= position[:, None])
    scale = 1.0 / HEAD_DIM ** 0.5

    def one_head(packed):
        q_head, k_head, v_head = packed
        scores = jnp.dot(q_head, k_head.T, preferred_element_type=jnp.float32) * scale
        scores = jnp.where(allowed, scores, -jnp.inf)
        top = lax.optimization_barrier(jnp.max(scores, axis=-1, keepdims=True))
        expo = jnp.exp(scores - top)
        probs = (expo / lax.optimization_barrier(jnp.sum(expo, axis=-1, keepdims=True))).astype(jnp.bfloat16)
        return jnp.dot(probs, v_head, preferred_element_type=jnp.float32)
    attended = lax.map(one_head, (q_all, k_all, v_all))
    attended = attended.transpose(1, 0, 2).reshape(count, HEADS * HEAD_DIM)
    center = attended - lax.optimization_barrier(jnp.mean(attended, axis=-1, keepdims=True))
    var = lax.optimization_barrier(jnp.mean(center * center, axis=-1, keepdims=True))
    normed = (center * lax.rsqrt(var + 1e-05) * sub_gain + sub_bias).astype(jnp.bfloat16)
    width = HEADS * HEAD_DIM // N_TENSOR
    projected = jnp.zeros((count, D), jnp.float32)
    for block in range(N_TENSOR):
        share = jnp.dot(normed[:, block * width:(block + 1) * width], out_weight[block * width:(block + 1) * width], preferred_element_type=jnp.float32)
        share = lax.optimization_barrier(share.astype(jnp.bfloat16))
        projected = projected + share.astype(jnp.float32)
    mixed = deep_alpha * residual.astype(jnp.float32) + projected
    centered = mixed - lax.optimization_barrier(jnp.mean(mixed, axis=-1, keepdims=True))
    spread = lax.optimization_barrier(jnp.mean(centered * centered, axis=-1, keepdims=True))
    return (centered * lax.rsqrt(spread + 1e-05) * post_gain + post_bias).astype(jnp.bfloat16)
```

```python
import functools

import jax
import jax.numpy as jnp
from jax import lax
from jax.experimental import pallas as pl
from jax.experimental.pallas import tpu as pltpu
from jax.sharding import PartitionSpec as P

HEAD_DIM = 128
TILE = 128
D = 4096
NY = 4
FEAT = 1024
NC = 4
CW = FEAT // NC
HPC = CW // HEAD_DIM
WCH = 4
WROWS = 256 // WCH
JC = 4
COL = 2048 // JC
WINDOW = (2, 4, 5, 5)
MESH = pl.DeviceIdType.MESH

deep_alpha = 160.0**0.25
LOG2E = 1.4426950408889634
SCALE = LOG2E / HEAD_DIM**0.5


def kernel(
    q, k, v, seg, res, gain, bias, w, pg, pb,
    out,
    qb, kb, vb, wb, gb, bb, mask, att, normed, stat, pbuf,
    oppb, rel, held, outb, fin, mixed, resb, pgb, pbb,
    loc_sem, y_send, y_recv, x_send, x_recv, w_send, w_recv, c_send, c_recv,
    g_send, g_recv, s_send, s_recv, o_send, o_recv, f_send, f_recv,
):
    dp = lax.axis_index("dp")
    t = lax.axis_index("tensor")
    core, hi, z = dp % 2, (dp // 2) % 2, dp // 4
    x, y = t % 2, t // 2

    def y_dev(d):
        return {"dp": dp, "tensor": ((y + d) % NY) * 2 + x}

    x_dev = {"dp": dp, "tensor": y * 2 + (1 - x)}
    wrap_dev = {"dp": z * 4 + (1 - hi) * 2 + core, "tensor": y * 2 + (1 - x)}
    core_dev = {"dp": z * 4 + hi * 2 + (1 - core), "tensor": t}

    def remote(src, dst, ss, rs, dev):
        return pltpu.make_async_remote_copy(
            src_ref=src, dst_ref=dst, send_sem=ss, recv_sem=rs, device_id=dev, device_id_type=MESH
        )

    def tile_rows(ty):
        return pl.ds(pl.multiple_of((2 * ty + x) * TILE, TILE), TILE)

    def cols(ty, c):
        return pl.ds(pl.multiple_of(ty * FEAT + c * CW, CW), CW)

    def y_copy(d, c, a):
        src = (q, k, v)[a].at[:, cols((y + d) % NY, c)]
        if a == 0:
            dst = qb.at[c, pl.ds(pl.multiple_of(y * TILE, TILE), TILE)]
        else:
            dst = (kb, vb)[a - 1].at[c, tile_rows(y)]
        return remote(src, dst, y_send.at[d - 1, c, a], y_recv.at[d - 1, c, a], y_dev(d))

    def x_copy(d, c, a):
        rows = tile_rows((y - d + NY) % NY)
        dst = (kb, vb)[a].at[c, rows]
        src = (k, v)[a].at[:, cols(y, c)] if d == 0 else dst
        return remote(src, dst, x_send.at[d, c, a], x_recv.at[d, c, a], x_dev)

    def x_recv_copy(d, c, a):
        ty = (y - d + NY) % NY
        rows = pl.ds(pl.multiple_of((2 * ty + 1 - x) * TILE, TILE), TILE)
        dst = (kb, vb)[a].at[c, rows]
        return remote(dst, dst, x_send.at[d, c, a], x_recv.at[d, c, a], x_dev)

    def y_recv_copy(d, c, a):
        ty = (y - d + NY) % NY
        if a == 0:
            dst = qb.at[c, pl.ds(pl.multiple_of(ty * TILE, TILE), TILE)]
        else:
            dst = (kb, vb)[a - 1].at[c, tile_rows(ty)]
        return remote(dst, dst, y_send.at[d - 1, c, a], y_recv.at[d - 1, c, a], y_dev(d))

    def own_copy(c, a):
        src = (q, k, v)[a].at[:, cols(y, c)]
        if a == 0:
            dst = qb.at[c, pl.ds(pl.multiple_of(y * TILE, TILE), TILE)]
        else:
            dst = (kb, vb)[a - 1].at[c, tile_rows(y)]
        return pltpu.make_async_copy(src, dst, loc_sem.at[c * 3 + a])

    def w_rows(owner, n, of_core):
        return pl.ds(pl.multiple_of(owner * 512 + of_core * 256 + n * WROWS, WROWS), WROWS)

    def w_copy(n):
        src = w.at[pl.ds(pl.multiple_of(core * 256 + n * WROWS, WROWS), WROWS)]
        return remote(src, wb.at[w_rows(x, n, core)], w_send.at[n], w_recv.at[n], wrap_dev)

    def w_recv_copy(n):
        dst = wb.at[w_rows(1 - x, n, core)]
        return remote(dst, dst, w_send.at[n], w_recv.at[n], wrap_dev)

    def c_copy(n):
        src = wb.at[w_rows(1 - x, n, core)]
        return remote(src, src, c_send.at[n], c_recv.at[n], core_dev)

    def c_recv_copy(n):
        dst = wb.at[w_rows(1 - x, n, 1 - core)]
        return remote(dst, dst, c_send.at[n], c_recv.at[n], core_dev)

    def g_copy(i):
        return remote((gain, bias)[i], (gb, bb)[i].at[x], g_send.at[i], g_recv.at[i], wrap_dev)

    def g_recv_copy(i):
        dst = (gb, bb)[i].at[1 - x]
        return remote(dst, dst, g_send.at[i], g_recv.at[i], wrap_dev)

    local = [own_copy(c, a) for c in range(NC) for a in range(3)]
    base = NC * 3
    local.append(
        pltpu.make_async_copy(
            w, wb.at[pl.ds(pl.multiple_of(x * 512, 512), 512)], loc_sem.at[base]
        )
    )
    local.append(pltpu.make_async_copy(gain, gb.at[x], loc_sem.at[base + 1]))
    local.append(pltpu.make_async_copy(bias, bb.at[x], loc_sem.at[base + 2]))
    local.append(pltpu.make_async_copy(res, resb, loc_sem.at[base + 3]))
    local.append(pltpu.make_async_copy(pg, pgb, loc_sem.at[base + 4]))
    local.append(pltpu.make_async_copy(pb, pbb, loc_sem.at[base + 5]))

    barrier = pltpu.get_barrier_semaphore()
    peers = [y_dev(1), y_dev(2), y_dev(3), x_dev, wrap_dev, core_dev]
    for dev in peers:
        pl.semaphore_signal(barrier, inc=1, device_id=dev, device_id_type=MESH)
    pl.semaphore_wait(barrier, len(peers))

    def send_first(c, carry):
        for d in (1, 3, 2):
            for a in (1, 2, 0):
                y_copy(d, c, a).start()
        for a in range(2):
            x_copy(0, c, a).start()
        w_copy(c).start()
        return carry

    lax.fori_loop(0, NC, send_first, 0)
    for i in range(2):
        g_copy(i).start()
    for copy in local:
        copy.start()

    for qi in range(NY):
        tq = 2 * qi + x
        first = (0, 0, x, 2 + x)[qi]
        row = seg[pl.ds(tq, 1), :].astype(jnp.float32)
        of_query = jnp.broadcast_to(row, (TILE, TILE)).T
        sub = lax.broadcasted_iota(jnp.int32, (TILE, TILE), 0) + tq * TILE
        lane = lax.broadcasted_iota(jnp.int32, (TILE, TILE), 1)
        for n in range(WINDOW[qi]):
            of_key = seg[pl.ds(first + n, 1), :].astype(jnp.float32)
            seen = (of_query == of_key) & (lane + (first + n) * TILE <= sub)
            mask[qi, :, n * TILE : (n + 1) * TILE] = jnp.where(seen, 0.0, -1e30)

    for copy in local:
        copy.wait()

    def receive_y(c):
        for d in (1, 3, 2):
            for a in (1, 2, 0):
                y_recv_copy(d, c, a).wait_recv()
        for d in (1, 3, 2):
            for a in range(2):
                x_copy(d, c, a).start()

    def attend(c):
        for d in range(NY):
            for a in range(2):
                x_recv_copy(d, c, a).wait_recv()
        for h in range(HPC):
            hc = pl.ds(h * HEAD_DIM, HEAD_DIM)
            for qi in range(NY):
                n = WINDOW[qi] * TILE
                first = (0, 0, x, 2 + x)[qi]
                keys = pl.ds(pl.multiple_of(first * TILE, TILE), n)
                rows = pl.ds(qi * TILE, TILE)
                s = lax.dot_general(
                    qb[c, rows, hc], kb[c, keys, hc], (((1,), (1,)), ((), ())),
                    preferred_element_type=jnp.float32,
                )
                s = s + mask[qi, :, :n]
                top = jnp.max(s, axis=-1, keepdims=True)
                p = jnp.exp2((s - top) * SCALE)
                total = jnp.sum(p, axis=-1, keepdims=True)
                o = jnp.dot(
                    p.astype(jnp.bfloat16), vb[c, keys, hc], preferred_element_type=jnp.float32
                )
                att[c, rows, hc] = o / total

    def forward_w(n):
        w_recv_copy(n).wait_recv()
        c_copy(n).start()

    receive_y(0)

    def chunk_step(c, carry):
        receive_y(c)
        forward_w(c - 1)
        attend(c - 1)
        return carry

    lax.fori_loop(1, NC, chunk_step, 0)
    forward_w(WCH - 1)
    attend(NC - 1)

    pad = lax.broadcasted_iota(jnp.int32, (TILE, TILE), 1)
    for qi in range(NY):
        rows = pl.ds(qi * TILE, TILE)
        mean = sum(jnp.sum(att[c, rows, :], axis=-1, keepdims=True) for c in range(NC)) / FEAT
        spread = sum(
            jnp.sum((att[c, rows, :] - mean) ** 2, axis=-1, keepdims=True) for c in range(NC)
        )
        both = jnp.where(pad == 0, mean, spread).T
        stat[0, qi] = both[:8]

    def s_copy(d):
        return remote(stat.at[0], stat.at[d], s_send.at[d - 1], s_recv.at[d - 1], y_dev(d))

    for d in (1, 2, 3):
        s_copy(d).start()
    for i in range(2):
        g_recv_copy(i).wait_recv()
    for d in (1, 2, 3):
        s_copy(d).wait_recv()
    for qi in range(NY):
        rows = pl.ds(qi * TILE, TILE)
        means = [stat[d, qi, 0:1, :] for d in range(NY)]
        mean = sum(means) / NY
        spread = sum(stat[d, qi, 1:2, :] for d in range(NY))
        spread = spread + FEAT * sum((m - mean) ** 2 for m in means)
        inv = lax.rsqrt(spread / (NY * FEAT) + 1e-05)
        sub = lax.broadcasted_iota(jnp.int32, (TILE, TILE), 0)
        both = jnp.where(sub == 0, mean, inv).T
        mean, inv = both[:, 0:1], both[:, 1:2]
        for c in range(NC):
            half = c * CW // 512
            lanes = pl.ds(c * CW % 512, CW)
            value = (att[c, rows, :] - mean) * inv * gb[half, :, lanes] + bb[half, :, lanes]
            normed[rows, c * CW : (c + 1) * CW] = value.astype(jnp.bfloat16)

    for n in range(WCH):
        c_recv_copy(n).wait_recv()

    def o_copy(half, j):
        return remote(
            oppb.at[half, j], rel.at[half, j], o_send.at[half, j], o_recv.at[half, j],
            y_dev(1 if half == 0 else 3),
        )

    def f_copy(way, half, j):
        return remote(
            outb.at[way, half, j], fin.at[way, half, j], f_send.at[way, half, j],
            f_recv.at[way, half, j], y_dev(1 if way == 0 else 3),
        )

    def rows_of(d):
        return pl.ds(pl.multiple_of(((y + d) % NY) * TILE, TILE), TILE)

    def project(j, carry):
        for half in range(2):
            col = pl.ds(pl.multiple_of(half * 2048 + j * COL, COL), COL)
            pbuf[...] = jnp.dot(normed[...], wb[:, col], preferred_element_type=jnp.float32)
            oppb[half, j] = pbuf[rows_of(2), :].astype(jnp.bfloat16)
            o_copy(half, j).start()
            way = 1 - half
            outb[way, half, j] = pbuf[rows_of(1 if way == 0 else 3), :].astype(jnp.bfloat16)
            f_copy(way, half, j).start()
            held[half, j] = pbuf[rows_of(1 if half == 0 else 3), :]
            mixed[half, j] = pbuf[rows_of(0), :] + deep_alpha * resb[:, col].astype(jnp.float32)
        return carry

    lax.fori_loop(0, JC, project, 0)

    def pass_on(j, carry):
        for half in range(2):
            o_copy(half, j).wait_recv()
            value = held[half, j] + rel[half, j].astype(jnp.float32)
            outb[half, half, j] = value.astype(jnp.bfloat16)
            f_copy(half, half, j).start()
        return carry

    lax.fori_loop(0, JC, pass_on, 0)

    def collect(j, total):
        for half in range(2):
            for way in range(2):
                f_copy(way, half, j).wait_recv()
            value = mixed[half, j] + fin[0, half, j].astype(jnp.float32)
            value = value + fin[1, half, j].astype(jnp.float32)
            mixed[half, j] = value
            total = total + jnp.sum(value, axis=-1, keepdims=True)
        return total

    total = lax.fori_loop(0, JC, collect, jnp.zeros((TILE, 1), jnp.float32))
    mean = total / D
    spread = jnp.zeros((TILE, 1), jnp.float32)
    for half in range(2):
        for j in range(JC):
            spread = spread + jnp.sum((mixed[half, j] - mean) ** 2, axis=-1, keepdims=True)
    inv = lax.rsqrt(spread / D + 1e-05)
    for half in range(2):
        for j in range(JC):
            col = pl.ds(half * 2048 + j * COL, COL)
            value = (mixed[half, j] - mean) * inv * pgb[:, col] + pbb[:, col]
            out[:, col] = value.astype(jnp.bfloat16)

    def sent(c, carry):
        for d in (1, 3, 2):
            for a in range(3):
                y_copy(d, c, a).wait_send()
        for d in range(NY):
            for a in range(2):
                x_copy(d, c, a).wait_send()
        w_copy(c).wait_send()
        c_copy(c).wait_send()
        return carry

    lax.fori_loop(0, NC, sent, 0)
    for i in range(2):
        g_copy(i).wait_send()
    for d in (1, 2, 3):
        s_copy(d).wait_send()

    def sent_shares(j, carry):
        for half in range(2):
            o_copy(half, j).wait_send()
            for way in range(2):
                f_copy(way, half, j).wait_send()
        return carry

    lax.fori_loop(0, JC, sent_shares, 0)


def body(
    queries, keys, values, segment_ids, residual, sub_gain, sub_bias, out_weight, post_gain, post_bias
):
    any_spec = pl.BlockSpec(memory_space=pl.ANY)
    vmem_spec = pl.BlockSpec(memory_space=pltpu.VMEM)
    bf16, f32 = jnp.bfloat16, jnp.float32
    dma = pltpu.SemaphoreType.DMA
    return pl.pallas_call(
        kernel,
        name="block",
        out_shape=jax.ShapeDtypeStruct((TILE, D), bf16),
        in_specs=[any_spec] * 3 + [vmem_spec] + [any_spec] * 6,
        out_specs=vmem_spec,
        scratch_shapes=[
            pltpu.VMEM((NC, NY * TILE, CW), bf16),
            pltpu.VMEM((NC, 8 * TILE, CW), bf16),
            pltpu.VMEM((NC, 8 * TILE, CW), bf16),
            pltpu.VMEM((FEAT, D), bf16),
            pltpu.VMEM((2, 1, 512), f32),
            pltpu.VMEM((2, 1, 512), f32),
            pltpu.VMEM((NY, TILE, 5 * TILE), f32),
            pltpu.VMEM((NC, NY * TILE, CW), f32),
            pltpu.VMEM((NY * TILE, FEAT), bf16),
            pltpu.VMEM((NY, NY, 8, TILE), f32),
            pltpu.VMEM((NY * TILE, COL), f32),
            pltpu.VMEM((2, JC, TILE, COL), bf16),
            pltpu.VMEM((2, JC, TILE, COL), bf16),
            pltpu.VMEM((2, JC, TILE, COL), f32),
            pltpu.VMEM((2, 2, JC, TILE, COL), bf16),
            pltpu.VMEM((2, 2, JC, TILE, COL), bf16),
            pltpu.VMEM((2, JC, TILE, COL), f32),
            pltpu.VMEM((TILE, D), bf16),
            pltpu.VMEM((1, D), f32),
            pltpu.VMEM((1, D), f32),
            dma((NC * 3 + 6,)),
            dma((3, NC, 3)),
            dma((3, NC, 3)),
            dma((NY, NC, 2)),
            dma((NY, NC, 2)),
            dma((WCH,)),
            dma((WCH,)),
            dma((WCH,)),
            dma((WCH,)),
            dma((2,)),
            dma((2,)),
            dma((3,)),
            dma((3,)),
            dma((2, JC)),
            dma((2, JC)),
            dma((2, 2, JC)),
            dma((2, 2, JC)),
        ],
        compiler_params=pltpu.CompilerParams(
            collective_id=0, has_side_effects=True, vmem_limit_bytes=56 << 20
        ),
    )(
        queries,
        keys,
        values,
        segment_ids.reshape(8, TILE),
        residual,
        sub_gain.reshape(1, 512),
        sub_bias.reshape(1, 512),
        out_weight,
        post_gain.reshape(1, D),
        post_bias.reshape(1, D),
    )


def solution(mesh):
    return jax.shard_map(
        body,
        mesh=mesh,
        in_specs=(
            P(("dp", "tensor"), None),
            P(("dp", "tensor"), None),
            P(("dp", "tensor"), None),
            P("dp"),
            P(("dp", "tensor"), None),
            P("tensor"),
            P("tensor"),
            P("tensor", None),
            P(),
            P(),
        ),
        out_specs=P(("dp", "tensor"), None),
        check_vma=False,
    )
```

```python
import jax
import jax.numpy as jnp
from jax import lax
from jax.experimental import pallas as pl
from jax.experimental.pallas import tpu as pltpu
from jax.sharding import PartitionSpec as P

HEAD_DIM = 128
TILE = 128
D = 4096
NY = 4
LATE = NY - 1
FEAT = 1024
NC = 8
CW = FEAT // NC
HPC = CW // HEAD_DIM
EARLY = 3 * NC // 8
WN = 4
WROWS = 128 // WN
JC = 4
COL = 2048 // JC
EXTRA = 16
ROWS = LATE * TILE + EXTRA
WINDOW = (2, 4, 5, 5)
MESH = pl.DeviceIdType.MESH

deep_alpha = 160.0**0.25
LOG2E = 1.4426950408889634
SCALE = LOG2E / HEAD_DIM**0.5


def kernel(
    q, k, v, seg, res, gain, bias, w, pg, pb,
    out,
    qb, kb, vb, wb, gb, bb, mask, att, left, left_late, stat, stat_in, vec, pbuf,
    oppb, rel, held, outb, fin, mixed, resb, pgb, pbb,
    loc_sem, y_send, y_recv, x_send, x_recv, w_send, w_recv, c_send, c_recv, z_send, z_recv,
    g_send, g_recv, s_send, s_recv, v_send, v_recv, o_send, o_recv, f_send, f_recv,
):
    dp = lax.axis_index("dp")
    t = lax.axis_index("tensor")
    core, hi, z = dp % 2, (dp // 2) % 2, dp // 4
    x, y = t % 2, t // 2
    zpar = z % 2

    def y_dev(ty):
        return {"dp": dp, "tensor": ty * 2 + x}

    x_dev = {"dp": dp, "tensor": y * 2 + (1 - x)}
    wrap_dev = {"dp": z * 4 + (1 - hi) * 2 + core, "tensor": y * 2 + (1 - x)}
    core_dev = {"dp": z * 4 + hi * 2 + (1 - core), "tensor": t}
    z_dev = {"dp": (z + 1 - 2 * zpar) * 4 + hi * 2 + core, "tensor": t}
    up, far, down = (y + 1) % NY, (y + 2) % NY, (y + 3) % NY

    def remote(src, dst, ss, rs, dev):
        return pltpu.make_async_remote_copy(
            src_ref=src, dst_ref=dst, send_sem=ss, recv_sem=rs, device_id=dev, device_id_type=MESH
        )

    def rows_at(n, size):
        return pl.ds(pl.multiple_of(n * size, size), size)

    def cols(ty, c):
        return pl.ds(pl.multiple_of(ty * FEAT + c * CW, CW), CW)

    def slot(a, ty, c):
        if a == 0:
            return qb.at[c, rows_at(ty, TILE)]
        return (kb, vb)[a - 1].at[c, rows_at(2 * ty + x, TILE)]

    def y_copy(n, c, a):
        ty = (y + n) % NY
        return remote(
            (q, k, v)[a].at[:, cols(ty, c)], slot(a, y, c),
            y_send.at[n - 1, c, a], y_recv.at[y, c, a], y_dev(ty),
        )

    def y_wait(ty, c, a):
        dst = slot(a, ty, c)
        remote(dst, dst, y_send.at[0, c, a], y_recv.at[ty, c, a], y_dev(ty)).wait_recv()

    def x_copy(ty, c, a):
        dst = slot(a, ty, c)
        return remote(dst, dst, x_send.at[ty, c, a - 1], x_recv.at[ty, c, a - 1], x_dev)

    def x_own(c, a):
        return remote(
            (q, k, v)[a].at[:, cols(y, c)], slot(a, y, c),
            x_send.at[y, c, a - 1], x_recv.at[y, c, a - 1], x_dev,
        )

    def x_wait(ty, c, a):
        dst = (kb, vb)[a - 1].at[c, rows_at(2 * ty + 1 - x, TILE)]
        remote(dst, dst, x_send.at[ty, c, a - 1], x_recv.at[ty, c, a - 1], x_dev).wait_recv()

    def piece(owner, of_core, of_z, n):
        return wb.at[rows_at(owner * 16 + of_core * 8 + of_z * 4 + n, WROWS)]

    def w_copy(n):
        src = w.at[rows_at(core * 8 + zpar * 4 + n, WROWS)]
        return remote(src, piece(x, core, zpar, n), w_send.at[n], w_recv.at[n], wrap_dev)

    def w_wait(n):
        dst = piece(1 - x, core, zpar, n)
        remote(dst, dst, w_send.at[n], w_recv.at[n], wrap_dev).wait_recv()

    def z_copy(n):
        src = piece(1 - x, core, zpar, n)
        return remote(src, src, z_send.at[n], z_recv.at[n], z_dev)

    def z_wait(n):
        dst = piece(1 - x, core, 1 - zpar, n)
        remote(dst, dst, z_send.at[n], z_recv.at[n], z_dev).wait_recv()

    def c_copy(of_z, n):
        src = piece(1 - x, core, of_z, n)
        return remote(src, src, c_send.at[of_z, n], c_recv.at[of_z, n], core_dev)

    def c_wait(of_z, n):
        dst = piece(1 - x, 1 - core, of_z, n)
        remote(dst, dst, c_send.at[of_z, n], c_recv.at[of_z, n], core_dev).wait_recv()

    def g_copy(i):
        return remote((gain, bias)[i], (gb, bb)[i].at[x], g_send.at[i], g_recv.at[i], wrap_dev)

    def g_wait(i):
        dst = (gb, bb)[i].at[1 - x]
        remote(dst, dst, g_send.at[i], g_recv.at[i], wrap_dev).wait_recv()

    def s_copy(ty):
        return remote(stat.at[ty], stat_in.at[y], s_send.at[ty], s_recv.at[y], y_dev(ty))

    def s_wait(ty):
        dst = stat_in.at[ty]
        remote(dst, dst, s_send.at[ty], s_recv.at[ty], y_dev(ty)).wait_recv()

    def v_copy(n):
        ty = (y + n) % NY
        return remote(vec.at[y], vec.at[y], v_send.at[n - 1], v_recv.at[y], y_dev(ty))

    def v_wait(ty):
        dst = vec.at[ty]
        remote(dst, dst, v_send.at[0], v_recv.at[ty], y_dev(ty)).wait_recv()

    def o_copy(half, j):
        return remote(
            oppb.at[half, j], rel.at[half, j], o_send.at[half, j], o_recv.at[half, j],
            y_dev((up, down)[half]),
        )

    def f_copy(way, half, j):
        return remote(
            outb.at[way, half, j], fin.at[way, half, j], f_send.at[way, half, j],
            f_recv.at[way, half, j], y_dev((up, down)[way]),
        )

    local = []

    def fetch(src, dst):
        local.append(pltpu.make_async_copy(src, dst, loc_sem.at[len(local)]))

    for c in range(NC):
        for a in range(3):
            fetch((q, k, v)[a].at[:, cols(y, c)], slot(a, y, c))
    fetch(gain, gb.at[x])
    fetch(bias, bb.at[x])
    fetch(pg, pgb)
    fetch(pb, pbb)
    fetch(res, resb)
    fetch(w, wb.at[rows_at(x, 512)])

    barrier = pltpu.get_barrier_semaphore()
    peers = [y_dev(up), y_dev(far), y_dev(down), x_dev, wrap_dev, core_dev, z_dev]
    for dev in peers:
        pl.semaphore_signal(barrier, inc=1, device_id=dev, device_id_type=MESH)
    pl.semaphore_wait(barrier, len(peers))

    def send_kv(c, carry):
        for n in (1, 3, 2):
            for a in (1, 2):
                y_copy(n, c, a).start()

        @pl.when((y != LATE) | ((x == 0) & (c < EARLY)))
        def _():
            for a in (1, 2):
                x_own(c, a).start()

        return carry

    def send_q(c, carry):
        for n in (1, 3, 2):
            y_copy(n, c, 0).start()
        return carry

    lax.fori_loop(0, 1, send_kv, 0)
    for n in range(WN):
        w_copy(n).start()
    lax.fori_loop(1, NC, send_kv, 0)
    for i in range(2):
        g_copy(i).start()
    lax.fori_loop(0, NC, send_q, 0)
    for copy in local:
        copy.start()

    first_of = (0, 0, x, 2 + x)
    for qi in range(NY):
        tq = 2 * qi + x
        row = seg[pl.ds(tq, 1), :].astype(jnp.float32)
        of_query = jnp.broadcast_to(row, (TILE, TILE)).T
        sub = lax.broadcasted_iota(jnp.int32, (TILE, TILE), 0) + tq * TILE
        lane = lax.broadcasted_iota(jnp.int32, (TILE, TILE), 1)
        for n in range(WINDOW[qi]):
            of_key = seg[pl.ds(first_of[qi] + n, 1), :].astype(jnp.float32)
            seen = (of_query == of_key) & (lane + (first_of[qi] + n) * TILE <= sub)
            mask[qi, :, n * TILE : (n + 1) * TILE] = jnp.where(seen, 0.0, -1e30)

    for copy in local:
        copy.wait()

    def receive_kv(c):
        for ty in range(NY):

            @pl.when(ty != y)
            def _():
                for a in (1, 2):
                    y_wait(ty, c, a)
                    if ty != LATE:
                        x_copy(ty, c, a).start()

    def spread_z(n):
        z_wait(n)
        c_copy(1 - zpar, n).start()

    def relay(i, carry):
        for h in range(NC // WN):
            receive_kv(i * (NC // WN) + h)
        w_wait(i)
        c_copy(zpar, i).start()
        z_copy(i).start()

        @pl.when(i >= 2)
        def _():
            spread_z(i - 2)

        return carry

    lax.fori_loop(0, WN, relay, 0)

    def relay_late(c, carry):
        @pl.when((x == 0) & ((y != LATE) | (c >= EARLY)))
        def _():
            for a in (1, 2):
                x_copy(LATE, c, a).start()

        return carry

    lax.fori_loop(0, NC, relay_late, 0)

    def attend(c, tiles):
        for h in range(HPC):
            hc = pl.ds(h * HEAD_DIM, HEAD_DIM)
            for qi in tiles:
                n = WINDOW[qi] * TILE
                keys = pl.ds(pl.multiple_of(first_of[qi] * TILE, TILE), n)
                rows = pl.ds(qi * TILE, TILE)
                s = lax.dot_general(
                    qb[c, rows, hc], kb[c, keys, hc], (((1,), (1,)), ((), ())),
                    preferred_element_type=jnp.float32,
                )
                s = s + mask[qi, :, :n]
                top = jnp.max(s, axis=-1, keepdims=True)
                p = jnp.exp2((s - top) * SCALE)
                total = jnp.sum(p, axis=-1, keepdims=True)
                o = jnp.dot(
                    p.astype(jnp.bfloat16), vb[c, keys, hc], preferred_element_type=jnp.float32
                )
                att[c, rows, hc] = o / total

    def first_tiles(c, carry):
        for ty in range(NY):

            @pl.when(ty != y)
            def _():
                y_wait(ty, c, 0)

        for ty in range(LATE):
            for a in (1, 2):
                x_wait(ty, c, a)
        attend(c, range(LATE))

        @pl.when((c == NC // 4) | (c == NC // 2))
        def _():
            spread_z(2 + (c * 4) // NC - 1)

        return carry

    lax.fori_loop(0, NC, first_tiles, 0)

    lane = lax.broadcasted_iota(jnp.int32, (TILE, TILE), 1)

    def lanes_of(c):
        return c * CW // 512, pl.ds(c * CW % 512, CW)

    def center(qi, dst, at):
        rows = pl.ds(qi * TILE, TILE)
        mean = sum(jnp.sum(att[c, rows, :], axis=-1, keepdims=True) for c in range(NC)) / FEAT
        spread = jnp.zeros((TILE, 1), jnp.float32)
        for c in range(NC):
            half, lanes = lanes_of(c)
            value = att[c, rows, :] - mean
            spread = spread + jnp.sum(value * value, axis=-1, keepdims=True)
            dst[at : at + TILE, c * CW : (c + 1) * CW] = (value * gb[half, :, lanes]).astype(
                jnp.bfloat16
            )
        stat[qi] = jnp.where(lane == 0, mean, spread).T[:8]

        @pl.when(qi != y)
        def _():
            s_copy(qi).start()

        @pl.when(qi == y)
        def _():
            stat_in[y] = stat[qi]

    for i in range(2):
        g_wait(i)
    sub = lax.broadcasted_iota(jnp.int32, (EXTRA, CW), 0)
    for c in range(NC):
        half, lanes = lanes_of(c)
        value = jnp.zeros((EXTRA, CW), jnp.float32)
        for i in range(2):
            row = (gb, bb)[i][half, :, lanes]
            high = row.astype(jnp.bfloat16).astype(jnp.float32)
            value = jnp.where(sub == 2 * i, high, jnp.where(sub == 2 * i + 1, row - high, value))
        left[LATE * TILE : ROWS, c * CW : (c + 1) * CW] = value.astype(jnp.bfloat16)
    for qi in range(LATE):
        center(qi, left, qi * TILE)

    for of_z in range(2):
        for n in range(WN):
            c_wait(of_z, n)

    def col(half, j):
        return pl.ds(pl.multiple_of(half * 2048 + j * COL, COL), COL)

    def hand_out(role, half, j, rows, start):
        value = pbuf[rows, :]
        if role == 2:
            oppb[half, j] = value.astype(jnp.bfloat16)
            o_copy(half, j).start()
        elif role == 0:
            mixed[half, j] = value
        else:
            way = 0 if role == 1 else 1
            if half == way:
                held[half, j] = value
            else:
                outb[way, half, j] = value.astype(jnp.bfloat16)
                if start:
                    f_copy(way, half, j).start()

    def project(j, carry):
        for half in range(2):
            pbuf[...] = jnp.dot(left[...], wb[:, col(half, j)], preferred_element_type=jnp.float32)
            for role in (2, 1, 3, 0):
                ty = (y + role) % NY

                @pl.when(ty != LATE)
                def _():
                    hand_out(role, half, j, rows_at(ty, TILE), False)

            extra = pbuf[LATE * TILE : ROWS, :]
            vec[y, 0, :, col(half, j)] = extra[0:1] + extra[1:2]
            vec[y, 1, :, col(half, j)] = extra[2:3] + extra[3:4]
        return carry

    lax.fori_loop(0, JC, project, 0)

    def send_direct(j, carry):
        @pl.when(up != LATE)
        def _():
            f_copy(0, 1, j).start()

        @pl.when(down != LATE)
        def _():
            f_copy(1, 0, j).start()

        return carry

    lax.fori_loop(0, JC, send_direct, 0)
    for n in (1, 3, 2):
        v_copy(n).start()

    def last_tile(c, carry):
        @pl.when(x == 1)
        def _():
            for a in (1, 2):
                x_wait(LATE, c, a)

        attend(c, (LATE,))
        return carry

    lax.fori_loop(0, NC, last_tile, 0)
    center(LATE, left_late, 0)

    def project_late(j, carry):
        for half in range(2):
            pbuf[:TILE] = jnp.dot(
                left_late[...], wb[:, col(half, j)], preferred_element_type=jnp.float32
            )
            for role in (2, 1, 3, 0):

                @pl.when((y + role) % NY == LATE)
                def _():
                    hand_out(role, half, j, pl.ds(0, TILE), True)

        return carry

    lax.fori_loop(0, JC, project_late, 0)

    def pass_on(half, j):
        o_copy(half, j).wait_recv()
        value = held[half, j] + rel[half, j].astype(jnp.float32)
        outb[half, half, j] = value.astype(jnp.bfloat16)
        f_copy(half, half, j).start()

    def pass_first(j, carry):
        for half in range(2):

            @pl.when((up, down)[half] != LATE)
            def _():
                pass_on(half, j)

        return carry

    def pass_late(j, carry):
        for half in range(2):

            @pl.when((up, down)[half] == LATE)
            def _():
                pass_on(half, j)

        return carry

    lax.fori_loop(0, JC, pass_first, 0)
    lax.fori_loop(0, JC, pass_late, 0)

    for ty in range(NY):

        @pl.when(ty != y)
        def _():
            s_wait(ty)
            v_wait(ty)

    means = [stat_in[ty, 0:1, :] for ty in range(NY)]
    mean = sum(means) / NY
    spread = sum(stat_in[ty, 1:2, :] for ty in range(NY))
    spread = spread + FEAT * sum((m - mean) ** 2 for m in means)
    inv = lax.rsqrt(spread / (NY * FEAT) + 1e-05)
    sub = lax.broadcasted_iota(jnp.int32, (TILE, TILE), 0)
    both = jnp.broadcast_to(inv, (TILE, TILE))
    for ty in range(NY):
        both = jnp.where(sub == ty, means[ty] - mean, both)
    both = both.T
    inv = both[:, NY : NY + 1]

    def prepare(j, carry):
        for half in range(2):
            value = mixed[half, j]
            shift = jnp.zeros((1, COL), jnp.float32)
            for ty in range(NY):
                value = value + both[:, ty : ty + 1] * vec[ty, 0, :, col(half, j)]
                shift = shift + vec[ty, 1, :, col(half, j)]
            stream = deep_alpha * resb[:, col(half, j)].astype(jnp.float32)
            mixed[half, j] = value * inv + shift + stream
        return carry

    lax.fori_loop(0, JC, prepare, 0)

    def collect(j, total):
        for half in range(2):
            for way in range(2):
                f_copy(way, half, j).wait_recv()
            value = fin[0, half, j].astype(jnp.float32) + fin[1, half, j].astype(jnp.float32)
            value = mixed[half, j] + inv * value
            mixed[half, j] = value
            total = total + jnp.sum(value, axis=-1, keepdims=True)
        return total

    total = lax.fori_loop(0, JC, collect, jnp.zeros((TILE, 1), jnp.float32))
    mean = total / D
    spread = jnp.zeros((TILE, 1), jnp.float32)
    for half in range(2):
        for j in range(JC):
            spread = spread + jnp.sum((mixed[half, j] - mean) ** 2, axis=-1, keepdims=True)
    inv = lax.rsqrt(spread / D + 1e-05)
    for half in range(2):
        for j in range(JC):
            lanes = pl.ds(half * 2048 + j * COL, COL)
            value = (mixed[half, j] - mean) * inv * pgb[:, lanes] + pbb[:, lanes]
            out[:, lanes] = value.astype(jnp.bfloat16)

    def sent(c, carry):
        for n in (1, 2, 3):
            for a in range(3):
                y_copy(n, c, a).wait_send()
        for ty in range(NY):

            @pl.when((ty != LATE) | (x == 0))
            def _():
                for a in (1, 2):
                    x_copy(ty, c, a).wait_send()

        return carry

    lax.fori_loop(0, NC, sent, 0)
    for n in range(WN):
        w_copy(n).wait_send()
        z_copy(n).wait_send()
        for of_z in range(2):
            c_copy(of_z, n).wait_send()
    for i in range(2):
        g_copy(i).wait_send()
    for ty in range(NY):

        @pl.when(ty != y)
        def _():
            s_copy(ty).wait_send()

    for n in (1, 2, 3):
        v_copy(n).wait_send()

    def sent_shares(j, carry):
        for half in range(2):
            o_copy(half, j).wait_send()
            for way in range(2):
                f_copy(way, half, j).wait_send()
        return carry

    lax.fori_loop(0, JC, sent_shares, 0)


def body(
    queries, keys, values, segment_ids, residual, sub_gain, sub_bias, out_weight, post_gain, post_bias
):
    any_spec = pl.BlockSpec(memory_space=pl.ANY)
    vmem_spec = pl.BlockSpec(memory_space=pltpu.VMEM)
    bf16, f32 = jnp.bfloat16, jnp.float32
    dma = pltpu.SemaphoreType.DMA
    return pl.pallas_call(
        kernel,
        name="block",
        out_shape=jax.ShapeDtypeStruct((TILE, D), bf16),
        in_specs=[any_spec] * 3 + [vmem_spec] + [any_spec] * 6,
        out_specs=vmem_spec,
        scratch_shapes=[
            pltpu.VMEM((NC, NY * TILE, CW), bf16),
            pltpu.VMEM((NC, 8 * TILE, CW), bf16),
            pltpu.VMEM((NC, 8 * TILE, CW), bf16),
            pltpu.VMEM((FEAT, D), bf16),
            pltpu.VMEM((2, 1, 512), f32),
            pltpu.VMEM((2, 1, 512), f32),
            pltpu.VMEM((NY, TILE, 5 * TILE), f32),
            pltpu.VMEM((NC, NY * TILE, CW), f32),
            pltpu.VMEM((ROWS, FEAT), bf16),
            pltpu.VMEM((TILE, FEAT), bf16),
            pltpu.VMEM((NY, 8, TILE), f32),
            pltpu.VMEM((NY, 8, TILE), f32),
            pltpu.VMEM((NY, 2, 1, D), f32),
            pltpu.VMEM((ROWS, COL), f32),
            pltpu.VMEM((2, JC, TILE, COL), bf16),
            pltpu.VMEM((2, JC, TILE, COL), bf16),
            pltpu.VMEM((2, JC, TILE, COL), f32),
            pltpu.VMEM((2, 2, JC, TILE, COL), bf16),
            pltpu.VMEM((2, 2, JC, TILE, COL), bf16),
            pltpu.VMEM((2, JC, TILE, COL), f32),
            pltpu.VMEM((TILE, D), bf16),
            pltpu.VMEM((1, D), f32),
            pltpu.VMEM((1, D), f32),
            dma((NC * 3 + 6,)),
            dma((3, NC, 3)),
            dma((NY, NC, 3)),
            dma((NY, NC, 2)),
            dma((NY, NC, 2)),
            dma((WN,)),
            dma((WN,)),
            dma((2, WN)),
            dma((2, WN)),
            dma((WN,)),
            dma((WN,)),
            dma((2,)),
            dma((2,)),
            dma((NY,)),
            dma((NY,)),
            dma((3,)),
            dma((NY,)),
            dma((2, JC)),
            dma((2, JC)),
            dma((2, 2, JC)),
            dma((2, 2, JC)),
        ],
        compiler_params=pltpu.CompilerParams(
            collective_id=0, has_side_effects=True, vmem_limit_bytes=56 << 20
        ),
    )(
        queries,
        keys,
        values,
        segment_ids.reshape(8, TILE),
        residual,
        sub_gain.reshape(1, 512),
        sub_bias.reshape(1, 512),
        out_weight,
        post_gain.reshape(1, D),
        post_bias.reshape(1, D),
    )


def solution(mesh):
    return jax.shard_map(
        body,
        mesh=mesh,
        in_specs=(
            P(("dp", "tensor"), None),
            P(("dp", "tensor"), None),
            P(("dp", "tensor"), None),
            P("dp"),
            P(("dp", "tensor"), None),
            P("tensor"),
            P("tensor"),
            P("tensor", None),
            P(),
            P(),
        ),
        out_specs=P(("dp", "tensor"), None),
        check_vma=False,
    )
```

```python
import jax
import jax.numpy as jnp
from jax import lax
from jax.experimental import pallas as pl
from jax.experimental.pallas import tpu as pltpu
from jax.sharding import PartitionSpec as P

HEAD_DIM = 128
TILE = 128
D = 4096
NY = 4
LATE = NY - 1
FEAT = 1024
NC = 8
CW = FEAT // NC
HALF = NC // 2
EARLY = 3 * NC // 8
WN = 4
WROWS = 128 // WN
JC = 4
COL = 2048 // JC
EXTRA = 16
ROWS = LATE * TILE + EXTRA
WINDOW = (2, 4, 5, 5)
MESH = pl.DeviceIdType.MESH

deep_alpha = 160.0**0.25
LOG2E = 1.4426950408889634
SCALE = LOG2E / HEAD_DIM**0.5


def kernel(
    q, k, v, seg_in, res, gain, bias, w, pg, pb,
    out,
    qb, kb, vb, wb, gb, mask, att, cen, acc, left, left_late, stat, stat_in, vec, pbuf,
    oppb, rel, held, outb, fin, mixed, final, resb, pgb, pbb, seg,
    loc_sem, sent_sem, kv_recv, q_recv, x_recv, l_recv, w_recv, z_recv, o_recv, f_recv, once_recv,
):
    dp = lax.axis_index("dp")
    t = lax.axis_index("tensor")
    core, hi, z = dp % 2, (dp // 2) % 2, dp // 4
    x, y = t % 2, t // 2
    zpar = z % 2

    def y_dev(ty):
        return {"dp": dp, "tensor": ty * 2 + x}

    x_dev = {"dp": dp, "tensor": y * 2 + (1 - x)}
    wrap_dev = {"dp": z * 4 + (1 - hi) * 2 + core, "tensor": y * 2 + (1 - x)}
    core_dev = {"dp": z * 4 + hi * 2 + (1 - core), "tensor": t}
    z_dev = {"dp": (z + 1 - 2 * zpar) * 4 + hi * 2 + core, "tensor": t}
    up, far, down = (y + 1) % NY, (y + 2) % NY, (y + 3) % NY

    def remote(src, dst, ss, rs, dev):
        return pltpu.make_async_remote_copy(
            src_ref=src, dst_ref=dst, send_sem=ss, recv_sem=rs, device_id=dev, device_id_type=MESH
        )

    def wait_bytes(ref, sem):
        pltpu.make_async_copy(ref, ref, sem).wait()

    def rows_at(n, size):
        return pl.ds(pl.multiple_of(n * size, size), size)

    def cols(ty, c):
        return pl.ds(pl.multiple_of(ty * FEAT + c * CW, CW), CW)

    def slot(a, ty, c):
        if a == 0:
            return qb.at[c, rows_at(ty, TILE)]
        return (kb, vb)[a - 1].at[c, rows_at(2 * ty + x, TILE)]

    def y_copy(n, c, a):
        ty = (y + n) % NY
        sem = q_recv if a == 0 else kv_recv
        return remote(
            (q, k, v)[a].at[:, cols(ty, c)], slot(a, y, c), sent_sem.at[0], sem.at[c], y_dev(ty)
        )

    def x_copy(ty, c, a):
        dst = slot(a, ty, c)
        return remote(dst, dst, sent_sem.at[1], x_recv.at[c], x_dev)

    def x_own(c, a):
        return remote(
            (q, k, v)[a].at[:, cols(y, c)], slot(a, y, c), sent_sem.at[1], x_recv.at[c], x_dev
        )

    def l_copy(c, a):
        dst = slot(a, LATE, c)
        return remote(dst, dst, sent_sem.at[2], l_recv.at[c // 2], x_dev)

    def l_own(c, a):
        return remote(
            (q, k, v)[a].at[:, cols(y, c)], slot(a, y, c), sent_sem.at[2], l_recv.at[c // 2], x_dev
        )

    def piece(owner, of_core, of_z, n):
        return wb.at[rows_at(owner * 16 + of_core * 8 + of_z * 4 + n, WROWS)]

    def w_copy(n):
        src = w.at[rows_at(core * 8 + zpar * 4 + n, WROWS)]
        return remote(src, piece(x, core, zpar, n), sent_sem.at[3], w_recv.at[n], wrap_dev)

    def w_wait(n):
        wait_bytes(piece(1 - x, core, zpar, n), w_recv.at[n])

    def z_copy(n):
        src = piece(1 - x, core, zpar, n)
        return remote(src, src, sent_sem.at[3], z_recv.at[n], z_dev)

    def z_wait(n):
        wait_bytes(piece(1 - x, core, 1 - zpar, n), z_recv.at[n])

    def c_copy(of_z, n):
        src = piece(1 - x, core, of_z, n)
        return remote(src, src, sent_sem.at[3], once_recv.at[0], core_dev)

    def g_copy(i):
        return remote((gain, bias)[i], gb.at[i, x], sent_sem.at[4], once_recv.at[1], wrap_dev)

    def s_copy(ty):
        return remote(stat.at[ty], stat_in.at[y], sent_sem.at[5], once_recv.at[2], y_dev(ty))

    def v_copy(n):
        return remote(vec.at[y], vec.at[y], sent_sem.at[6], once_recv.at[3], y_dev((y + n) % NY))

    def o_copy(half, j):
        return remote(
            oppb.at[half, j], rel.at[half, j], sent_sem.at[7], o_recv.at[half, j],
            y_dev((up, down)[half]),
        )

    def f_copy(way, half, j):
        return remote(
            outb.at[way, half, j], fin.at[way, half, j], sent_sem.at[8],
            f_recv.at[half, j], y_dev((up, down)[way]),
        )

    def fetch(src, dst, n):
        return pltpu.make_async_copy(src, dst, loc_sem.at[n])

    fetch_seg = fetch(seg_in, seg, 0)
    fetch_seg.start()

    barrier = pltpu.get_barrier_semaphore()
    peers = [y_dev(up), y_dev(far), y_dev(down), x_dev, wrap_dev, core_dev, z_dev]
    for dev in peers:
        pl.semaphore_signal(barrier, inc=1, device_id=dev, device_id_type=MESH)
    pl.semaphore_wait(barrier, len(peers))

    def send_kv(c, carry):
        for n in (1, 3, 2):
            for a in (1, 2):
                y_copy(n, c, a).start()

        @pl.when(y != LATE)
        def _():
            for a in (1, 2):
                x_own(c, a).start()

        @pl.when((y == LATE) & (x == 0) & (c < EARLY))
        def _():
            for a in (1, 2):
                l_own(c, a).start()

        return carry

    def send_q(c, carry):
        for n in (1, 3, 2):
            y_copy(n, c, 0).start()
        return carry

    lax.fori_loop(0, 1, send_kv, 0)
    for n in range(WN):
        w_copy(n).start()
    lax.fori_loop(1, NC, send_kv, 0)
    for i in range(2):
        g_copy(i).start()
    lax.fori_loop(0, NC, send_q, 0)

    def fetch_own(c, carry):
        for a in range(3):
            fetch((q, k, v)[a].at[:, cols(y, c)], slot(a, y, c), 1).start()
        return carry

    lax.fori_loop(0, NC, fetch_own, 0)
    fetch_gains = [fetch(gain, gb.at[0, x], 2), fetch(bias, gb.at[1, x], 2)]
    fetch_w = fetch(w, wb.at[rows_at(x, 512)], 3)
    fetch_rest = [fetch(pg, pgb, 4), fetch(pb, pbb, 5), fetch(res, resb, 6)]
    for copy in fetch_gains + [fetch_w] + fetch_rest:
        copy.start()

    fetch_seg.wait()

    first_of = (0, 0, x, 2 + x)
    for qi in range(NY):
        tq = 2 * qi + x
        row = seg[pl.ds(tq, 1), :].astype(jnp.float32)
        of_query = jnp.broadcast_to(row, (TILE, TILE)).T
        sub = lax.broadcasted_iota(jnp.int32, (TILE, TILE), 0) + tq * TILE
        lane = lax.broadcasted_iota(jnp.int32, (TILE, TILE), 1)
        for n in range(WINDOW[qi]):
            of_key = seg[pl.ds(first_of[qi] + n, 1), :].astype(jnp.float32)
            seen = (of_query == of_key) & (lane + (first_of[qi] + n) * TILE <= sub)
            mask[qi, :, n * TILE : (n + 1) * TILE] = jnp.where(seen, 0.0, -1e30)

    wait_bytes(kb.at[0:3], loc_sem.at[1])

    def receive_kv(c):
        wait_bytes(kb.at[0, 0 : 6 * TILE], kv_recv.at[c])
        for ty in range(LATE):

            @pl.when(ty != y)
            def _():
                for a in (1, 2):
                    x_copy(ty, c, a).start()

    def spread_z(n):
        z_wait(n)
        c_copy(1 - zpar, n).start()

    def relay(i, carry):
        for h in range(NC // WN):
            receive_kv(i * (NC // WN) + h)
        w_wait(i)
        c_copy(zpar, i).start()
        z_copy(i).start()

        @pl.when(i >= 2)
        def _():
            spread_z(i - 2)

        return carry

    lax.fori_loop(0, WN, relay, 0)

    def relay_late(c, carry):
        @pl.when((x == 0) & ((y != LATE) | (c >= EARLY)))
        def _():
            for a in (1, 2):
                l_copy(c, a).start()

        return carry

    lax.fori_loop(0, NC, relay_late, 0)

    def gains(c):
        return gb[0, c // 4, :, pl.ds(pl.multiple_of((c % 4) * CW, CW), CW)]

    def put(value, c, qi, dst, at, first):
        rows = pl.ds(qi * TILE, TILE)
        value = value - cen[rows, :]
        lanes = pl.ds(pl.multiple_of(c * CW, CW), CW)
        dst[at : at + TILE, lanes] = (value * gains(c)).astype(jnp.bfloat16)
        if first:
            acc[0, rows, :] = value
            acc[1, rows, :] = value * value
        else:
            acc[0, rows, :] += value
            acc[1, rows, :] += value * value

    def attend(c, tiles, dst):
        for qi in tiles:
            n = WINDOW[qi] * TILE
            keys = pl.ds(pl.multiple_of(first_of[qi] * TILE, TILE), n)
            rows = pl.ds(qi * TILE, TILE)
            s = lax.dot_general(
                qb[c, rows, :], kb[c, keys, :], (((1,), (1,)), ((), ())),
                preferred_element_type=jnp.float32,
            )
            s = s + mask[qi, :, :n]
            top = jnp.max(s, axis=-1, keepdims=True)
            p = jnp.exp2((s - top) * SCALE)
            total = jnp.sum(p, axis=-1, keepdims=True)
            o = jnp.dot(
                p.astype(jnp.bfloat16), vb[c, keys, :], preferred_element_type=jnp.float32
            )
            o = o / total
            if dst is None:
                att[c, rows, :] = o
            else:
                put(o, c, qi, dst, (qi - tiles[0]) * TILE, False)

    def center(tiles, dst):
        for qi in tiles:
            rows = pl.ds(qi * TILE, TILE)
            mean = sum(att[c, rows, :] for c in range(HALF))
            mean = jnp.sum(mean, axis=-1, keepdims=True) / (HALF * CW)
            cen[rows, :] = jnp.broadcast_to(mean, (TILE, CW))
            for c in range(HALF):
                put(att[c, rows, :], c, qi, dst, (qi - tiles[0]) * TILE, c == 0)

    def attend_all(tiles, dst, wait):
        def first_half(c, carry):
            wait(c)
            attend(c, tiles, None)
            return carry

        def second_half(c, carry):
            wait(c)
            attend(c, tiles, dst)
            return carry

        lax.fori_loop(0, HALF, first_half, 0)
        center(tiles, dst)
        lax.fori_loop(HALF, NC, second_half, 0)

    def wait_first(c):
        wait_bytes(kb.at[0, 0 : 3 * TILE], q_recv.at[c])
        wait_bytes(kb.at[0, 0 : 6 * TILE], x_recv.at[c])

        @pl.when((c == 2) | (c == 4))
        def _():
            spread_z(1 + c // 2)

    def wait_last(c):
        @pl.when((x == 1) & (c % 2 == 0))
        def _():
            wait_bytes(kb.at[0, 0 : 4 * TILE], l_recv.at[c // 2])

    lane = lax.broadcasted_iota(jnp.int32, (TILE, TILE), 1)

    def statistics(qi):
        rows = pl.ds(qi * TILE, TILE)
        mid = cen[rows, 0:1]
        shift = jnp.sum(acc[0, rows, :], axis=-1, keepdims=True)
        spread = jnp.sum(acc[1, rows, :], axis=-1, keepdims=True) - shift * shift / FEAT
        mean = mid + shift / FEAT
        stat[qi] = jnp.where(lane == 0, mid, jnp.where(lane == 1, mean, spread)).T[:8]

        @pl.when(qi != y)
        def _():
            s_copy(qi).start()

        @pl.when(qi == y)
        def _():
            stat_in[y] = stat[qi]

    for copy in fetch_gains:
        copy.wait()
    wait_bytes(gb.at[:, 0], once_recv.at[1])
    sub = lax.broadcasted_iota(jnp.int32, (EXTRA, CW), 0)
    for c in range(NC):
        half, lanes = c * CW // 512, pl.ds(c * CW % 512, CW)
        value = jnp.zeros((EXTRA, CW), jnp.float32)
        for i in range(2):
            row = gb[i, half, :, lanes]
            high = row.astype(jnp.bfloat16).astype(jnp.float32)
            value = jnp.where(sub == 2 * i, high, jnp.where(sub == 2 * i + 1, row - high, value))
        left[LATE * TILE : ROWS, c * CW : (c + 1) * CW] = value.astype(jnp.bfloat16)

    attend_all(range(LATE), left, wait_first)

    fetch_w.wait()
    wait_bytes(kb, once_recv.at[0])

    def col(half, j):
        return pl.ds(pl.multiple_of(half * 2048 + j * COL, COL), COL)

    def hand_out(role, half, j, rows, start):
        value = pbuf[rows, :]
        if role == 2:
            oppb[half, j] = value.astype(jnp.bfloat16)
            o_copy(half, j).start()
        elif role == 0:
            mixed[half, j] = value
        else:
            way = 0 if role == 1 else 1
            if half == way:
                held[half, j] = value
            else:
                outb[way, half, j] = value.astype(jnp.bfloat16)
                if start:
                    f_copy(way, half, j).start()

    def project(j, carry):
        for half in range(2):
            pbuf[...] = jnp.dot(left[...], wb[:, col(half, j)], preferred_element_type=jnp.float32)
            for role in (2, 1, 3, 0):
                ty = (y + role) % NY

                @pl.when(ty != LATE)
                def _():
                    hand_out(role, half, j, rows_at(ty, TILE), False)

            extra = pbuf[LATE * TILE : ROWS, :]
            vec[y, 0, :, col(half, j)] = extra[0:1] + extra[1:2]
            vec[y, 1, :, col(half, j)] = extra[2:3] + extra[3:4]
        return carry

    lax.fori_loop(0, JC, project, 0)

    def send_direct(j, carry):
        @pl.when(up != LATE)
        def _():
            f_copy(0, 1, j).start()

        @pl.when(down != LATE)
        def _():
            f_copy(1, 0, j).start()

        return carry

    lax.fori_loop(0, JC, send_direct, 0)
    for n in (1, 3, 2):
        v_copy(n).start()
    for qi in range(LATE):
        statistics(qi)

    attend_all((LATE,), left_late, wait_last)

    def project_late(j, carry):
        for half in range(2):
            pbuf[:TILE] = jnp.dot(
                left_late[...], wb[:, col(half, j)], preferred_element_type=jnp.float32
            )
            for role in (2, 1, 3, 0):

                @pl.when((y + role) % NY == LATE)
                def _():
                    hand_out(role, half, j, pl.ds(0, TILE), True)

        return carry

    lax.fori_loop(0, JC, project_late, 0)

    statistics(LATE)
    wait_bytes(wb.at[0:288], sent_sem.at[0])
    wait_bytes(kb.at[0:6], sent_sem.at[1])

    @pl.when(x == 0)
    def _():
        wait_bytes(kb.at[0:2], sent_sem.at[2])

    wait_bytes(wb.at[0:512], sent_sem.at[3])
    wait_bytes(gb.at[:, 0], sent_sem.at[4])
    wait_bytes(stat.at[0:3], sent_sem.at[5])
    wait_bytes(vec.at[0:3], sent_sem.at[6])

    def pass_on(half, j):
        wait_bytes(rel.at[half, j], o_recv.at[half, j])
        value = held[half, j] + rel[half, j].astype(jnp.float32)
        outb[half, half, j] = value.astype(jnp.bfloat16)
        f_copy(half, half, j).start()

    def pass_first(j, carry):
        for half in range(2):

            @pl.when((up, down)[half] != LATE)
            def _():
                pass_on(half, j)

        return carry

    def pass_late(j, carry):
        for half in range(2):

            @pl.when((up, down)[half] == LATE)
            def _():
                pass_on(half, j)

        return carry

    lax.fori_loop(0, JC, pass_first, 0)
    lax.fori_loop(0, JC, pass_late, 0)

    wait_bytes(stat_in.at[0:3], once_recv.at[2])
    wait_bytes(vec.at[0:3], once_recv.at[3])
    for copy in fetch_rest:
        copy.wait()

    means = [stat_in[ty, 1:2, :] for ty in range(NY)]
    mean = sum(means) / NY
    spread = sum(stat_in[ty, 2:3, :] for ty in range(NY))
    spread = spread + FEAT * sum((m - mean) ** 2 for m in means)
    inv = lax.rsqrt(spread / (NY * FEAT) + 1e-05)
    sub = lax.broadcasted_iota(jnp.int32, (TILE, TILE), 0)
    both = jnp.broadcast_to(inv, (TILE, TILE))
    for ty in range(NY):
        both = jnp.where(sub == ty, stat_in[ty, 0:1, :] - mean, both)
    both = both.T
    inv = both[:, NY : NY + 1]

    def prepare(j, carry):
        for half in range(2):
            value = mixed[half, j]
            shift = jnp.zeros((1, COL), jnp.float32)
            for ty in range(NY):
                value = value + both[:, ty : ty + 1] * vec[ty, 0, :, col(half, j)]
                shift = shift + vec[ty, 1, :, col(half, j)]
            stream = deep_alpha * resb[:, col(half, j)].astype(jnp.float32)
            mixed[half, j] = value * inv + shift + stream
        return carry

    lax.fori_loop(0, JC, prepare, 0)

    def m_copy(half, j):
        return pltpu.make_async_copy(
            final.at[half, j], out.at[:, col(half, j)], loc_sem.at[7]
        )

    def collect(j, total):
        for half in range(2):
            wait_bytes(fin.at[:, half, j], f_recv.at[half, j])
            value = fin[0, half, j].astype(jnp.float32) + fin[1, half, j].astype(jnp.float32)
            value = mixed[half, j] + inv * value
            mixed[half, j] = value
            total = total + jnp.sum(value, axis=-1, keepdims=True)
        return total

    total = lax.fori_loop(0, JC, collect, jnp.zeros((TILE, 1), jnp.float32))
    mean = total / D
    spread = jnp.zeros((TILE, 1), jnp.float32)
    for half in range(2):
        for j in range(JC):
            spread = spread + jnp.sum((mixed[half, j] - mean) ** 2, axis=-1, keepdims=True)
    inv = lax.rsqrt(spread / D + 1e-05)
    for half in range(2):
        for j in range(JC):
            lanes = pl.ds(half * 2048 + j * COL, COL)
            value = (mixed[half, j] - mean) * inv * pgb[:, lanes] + pbb[:, lanes]
            final[half, j] = value.astype(jnp.bfloat16)
            m_copy(half, j).start()
    wait_bytes(final, loc_sem.at[7])
    wait_bytes(oppb, sent_sem.at[7])
    wait_bytes(outb, sent_sem.at[8])


def body(
    queries, keys, values, segment_ids, residual, sub_gain, sub_bias, out_weight, post_gain, post_bias
):
    any_spec = pl.BlockSpec(memory_space=pl.ANY)
    bf16, f32 = jnp.bfloat16, jnp.float32
    dma = pltpu.SemaphoreType.DMA
    return pl.pallas_call(
        kernel,
        name="block",
        out_shape=jax.ShapeDtypeStruct((TILE, D), bf16),
        in_specs=[any_spec] * 10,
        out_specs=any_spec,
        scratch_shapes=[
            pltpu.VMEM((NC, NY * TILE, CW), bf16),
            pltpu.VMEM((NC, 8 * TILE, CW), bf16),
            pltpu.VMEM((NC, 8 * TILE, CW), bf16),
            pltpu.VMEM((FEAT, D), bf16),
            pltpu.VMEM((2, 2, 1, 512), f32),
            pltpu.VMEM((NY, TILE, 5 * TILE), f32),
            pltpu.VMEM((HALF, NY * TILE, CW), f32),
            pltpu.VMEM((NY * TILE, CW), f32),
            pltpu.VMEM((2, NY * TILE, CW), f32),
            pltpu.VMEM((ROWS, FEAT), bf16),
            pltpu.VMEM((TILE, FEAT), bf16),
            pltpu.VMEM((NY, 8, TILE), f32),
            pltpu.VMEM((NY, 8, TILE), f32),
            pltpu.VMEM((NY, 2, 1, D), f32),
            pltpu.VMEM((ROWS, COL), f32),
            pltpu.VMEM((2, JC, TILE, COL), bf16),
            pltpu.VMEM((2, JC, TILE, COL), bf16),
            pltpu.VMEM((2, JC, TILE, COL), f32),
            pltpu.VMEM((2, 2, JC, TILE, COL), bf16),
            pltpu.VMEM((2, 2, JC, TILE, COL), bf16),
            pltpu.VMEM((2, JC, TILE, COL), f32),
            pltpu.VMEM((2, JC, TILE, COL), bf16),
            pltpu.VMEM((TILE, D), bf16),
            pltpu.VMEM((1, D), f32),
            pltpu.VMEM((1, D), f32),
            pltpu.VMEM((8, TILE), jnp.int32),
            dma((8,)),
            dma((9,)),
            dma((NC,)),
            dma((NC,)),
            dma((NC,)),
            dma((NC // 2,)),
            dma((WN,)),
            dma((WN,)),
            dma((2, JC)),
            dma((2, JC)),
            dma((4,)),
        ],
        compiler_params=pltpu.CompilerParams(
            collective_id=0, has_side_effects=True, vmem_limit_bytes=56 << 20
        ),
    )(
        queries,
        keys,
        values,
        segment_ids.reshape(8, TILE),
        residual,
        sub_gain.reshape(1, 512),
        sub_bias.reshape(1, 512),
        out_weight,
        post_gain.reshape(1, D),
        post_bias.reshape(1, D),
    )


def solution(mesh):
    return jax.shard_map(
        body,
        mesh=mesh,
        in_specs=(
            P(("dp", "tensor"), None),
            P(("dp", "tensor"), None),
            P(("dp", "tensor"), None),
            P("dp"),
            P(("dp", "tensor"), None),
            P("tensor"),
            P("tensor"),
            P("tensor", None),
            P(),
            P(),
        ),
        out_specs=P(("dp", "tensor"), None),
        check_vma=False,
    )
```

```python
import jax
import jax.numpy as jnp
from jax import lax
from jax.experimental import pallas as pl
from jax.experimental.pallas import tpu as pltpu
from jax.sharding import PartitionSpec as P

HEAD_DIM = 128
TILE = 128
D = 4096
NY = 4
LATE = NY - 1
FEAT = 1024
NC = 8
CW = FEAT // NC
HALF = NC // 2
EARLY = 3 * NC // 8
WN = 4
WROWS = 128 // WN
JC = 4
COL = 2048 // JC
EXTRA = 16
ROWS = LATE * TILE + EXTRA
WINDOW = (2, 4, 5, 5)
MESH = pl.DeviceIdType.MESH

deep_alpha = 160.0**0.25
LOG2E = 1.4426950408889634
SCALE = LOG2E / HEAD_DIM**0.5


def kernel(
    q, k, v, seg_in, res, gain, bias, w, pg, pb,
    out,
    qs, ks, vs, qb, kb, vb, wb, gb, mask, att, cen, acc, left, left_late, stat, stat_in, vec, pbuf,
    oppb, rel, held, outb, fin, mixed, final, resb, pgb, pbb, seg,
    loc_sem, sent_sem, kv_recv, q_recv, x_recv, l_recv, w_recv, z_recv, o_recv, f_recv, once_recv,
):
    dp = lax.axis_index("dp")
    t = lax.axis_index("tensor")
    core, hi, z = dp % 2, (dp // 2) % 2, dp // 4
    x, y = t % 2, t // 2
    zpar = z % 2

    def y_dev(ty):
        return {"dp": dp, "tensor": ty * 2 + x}

    x_dev = {"dp": dp, "tensor": y * 2 + (1 - x)}
    wrap_dev = {"dp": z * 4 + (1 - hi) * 2 + core, "tensor": y * 2 + (1 - x)}
    core_dev = {"dp": z * 4 + hi * 2 + (1 - core), "tensor": t}
    z_dev = {"dp": (z + 1 - 2 * zpar) * 4 + hi * 2 + core, "tensor": t}
    up, far, down = (y + 1) % NY, (y + 2) % NY, (y + 3) % NY

    def remote(src, dst, ss, rs, dev):
        return pltpu.make_async_remote_copy(
            src_ref=src, dst_ref=dst, send_sem=ss, recv_sem=rs, device_id=dev, device_id_type=MESH
        )

    def wait_bytes(ref, sem):
        pltpu.make_async_copy(ref, ref, sem).wait()

    def rows_at(n, size):
        return pl.ds(pl.multiple_of(n * size, size), size)

    def cols(ty, c):
        return pl.ds(pl.multiple_of(ty * FEAT + c * CW, CW), CW)

    def slot(a, ty, c):
        if a == 0:
            return qb.at[c, rows_at(ty, TILE)]
        return (kb, vb)[a - 1].at[c, rows_at(2 * ty + x, TILE)]

    def y_copy(n, c, a):
        ty = (y + n) % NY
        sem = q_recv if a == 0 else kv_recv
        return remote(
            (qs, ks, vs)[a].at[:, cols(ty, c)], slot(a, y, c), sent_sem.at[0], sem.at[c], y_dev(ty)
        )

    def x_copy(ty, c, a):
        dst = slot(a, ty, c)
        return remote(dst, dst, sent_sem.at[1], x_recv.at[c], x_dev)

    def x_own(c, a):
        return remote(
            (qs, ks, vs)[a].at[:, cols(y, c)], slot(a, y, c), sent_sem.at[1], x_recv.at[c], x_dev
        )

    def l_copy(c, a):
        dst = slot(a, LATE, c)
        return remote(dst, dst, sent_sem.at[2], l_recv.at[c // 2], x_dev)

    def l_own(c, a):
        return remote(
            (qs, ks, vs)[a].at[:, cols(y, c)], slot(a, y, c), sent_sem.at[2], l_recv.at[c // 2], x_dev
        )

    def piece(owner, of_core, of_z, n):
        return wb.at[rows_at(owner * 16 + of_core * 8 + of_z * 4 + n, WROWS)]

    def w_copy(n):
        src = w.at[rows_at(core * 8 + zpar * 4 + n, WROWS)]
        return remote(src, piece(x, core, zpar, n), sent_sem.at[3], w_recv.at[n], wrap_dev)

    def w_wait(n):
        wait_bytes(piece(1 - x, core, zpar, n), w_recv.at[n])

    def z_copy(n):
        src = piece(1 - x, core, zpar, n)
        return remote(src, src, sent_sem.at[3], z_recv.at[n], z_dev)

    def z_wait(n):
        wait_bytes(piece(1 - x, core, 1 - zpar, n), z_recv.at[n])

    def c_copy(of_z, n):
        src = piece(1 - x, core, of_z, n)
        return remote(src, src, sent_sem.at[3], once_recv.at[0], core_dev)

    def g_copy(i):
        return remote((gain, bias)[i], gb.at[i, x], sent_sem.at[4], once_recv.at[1], wrap_dev)

    def s_copy(ty):
        return remote(stat.at[ty], stat_in.at[y], sent_sem.at[5], once_recv.at[2], y_dev(ty))

    def v_copy(n):
        return remote(vec.at[y], vec.at[y], sent_sem.at[6], once_recv.at[3], y_dev((y + n) % NY))

    def o_copy(half, j):
        return remote(
            oppb.at[half, j], rel.at[half, j], sent_sem.at[7], o_recv.at[half, j],
            y_dev((up, down)[half]),
        )

    def f_copy(way, half, j):
        return remote(
            outb.at[way, half, j], fin.at[way, half, j], sent_sem.at[8],
            f_recv.at[half, j], y_dev((up, down)[way]),
        )

    def fetch(src, dst, n):
        return pltpu.make_async_copy(src, dst, loc_sem.at[n])

    stage = [fetch((q, k, v)[a], (qs, ks, vs)[a], 8 + a) for a in range(3)]
    for a in (1, 2, 0):
        stage[a].start()
    fetch_seg = fetch(seg_in, seg, 0)
    fetch_seg.start()

    barrier = pltpu.get_barrier_semaphore()
    peers = [y_dev(up), y_dev(far), y_dev(down), x_dev, wrap_dev, core_dev, z_dev]
    for dev in peers:
        pl.semaphore_signal(barrier, inc=1, device_id=dev, device_id_type=MESH)
    pl.semaphore_wait(barrier, len(peers))

    def send_kv(c, carry):
        for a in (1, 2):
            for n in (1, 3, 2):
                y_copy(n, c, a).start()

        @pl.when(y != LATE)
        def _():
            for a in (1, 2):
                x_own(c, a).start()

        @pl.when((y == LATE) & (x == 0) & (c < EARLY))
        def _():
            for a in (1, 2):
                l_own(c, a).start()

        return carry

    def send_q(c, carry):
        for n in (1, 3, 2):
            y_copy(n, c, 0).start()
        return carry

    stage[1].wait()
    stage[2].wait()
    lax.fori_loop(0, 1, send_kv, 0)
    for n in range(WN):
        w_copy(n).start()
    lax.fori_loop(1, NC, send_kv, 0)
    for i in range(2):
        g_copy(i).start()
    stage[0].wait()
    lax.fori_loop(0, NC, send_q, 0)

    def fetch_own(c, carry):
        for a in range(3):
            fetch((qs, ks, vs)[a].at[:, cols(y, c)], slot(a, y, c), 1).start()
        return carry

    lax.fori_loop(0, NC, fetch_own, 0)
    fetch_gains = [fetch(gain, gb.at[0, x], 2), fetch(bias, gb.at[1, x], 2)]
    fetch_w = fetch(w, wb.at[rows_at(x, 512)], 3)
    fetch_rest = [fetch(pg, pgb, 4), fetch(pb, pbb, 5), fetch(res, resb, 6)]
    for copy in fetch_gains + [fetch_w] + fetch_rest:
        copy.start()

    fetch_seg.wait()

    first_of = (0, 0, x, 2 + x)
    for qi in range(NY):
        tq = 2 * qi + x
        row = seg[pl.ds(tq, 1), :].astype(jnp.float32)
        of_query = jnp.broadcast_to(row, (TILE, TILE)).T
        sub = lax.broadcasted_iota(jnp.int32, (TILE, TILE), 0) + tq * TILE
        lane = lax.broadcasted_iota(jnp.int32, (TILE, TILE), 1)
        for n in range(WINDOW[qi]):
            of_key = seg[pl.ds(first_of[qi] + n, 1), :].astype(jnp.float32)
            seen = (of_query == of_key) & (lane + (first_of[qi] + n) * TILE <= sub)
            mask[qi, :, n * TILE : (n + 1) * TILE] = jnp.where(seen, 0.0, -1e30)

    wait_bytes(kb.at[0:3], loc_sem.at[1])

    def receive_kv(c):
        wait_bytes(kb.at[0, 0 : 6 * TILE], kv_recv.at[c])
        for ty in range(LATE):

            @pl.when(ty != y)
            def _():
                for a in (1, 2):
                    x_copy(ty, c, a).start()

    def spread_z(n):
        z_wait(n)
        c_copy(1 - zpar, n).start()

    def relay(i, carry):
        for h in range(NC // WN):
            receive_kv(i * (NC // WN) + h)
        w_wait(i)
        c_copy(zpar, i).start()
        z_copy(i).start()

        @pl.when(i >= 2)
        def _():
            spread_z(i - 2)

        return carry

    lax.fori_loop(0, WN, relay, 0)

    def relay_late(c, carry):
        @pl.when((x == 0) & ((y != LATE) | (c >= EARLY)))
        def _():
            for a in (1, 2):
                l_copy(c, a).start()

        return carry

    lax.fori_loop(0, NC, relay_late, 0)

    def gains(c):
        return gb[0, c // 4, :, pl.ds(pl.multiple_of((c % 4) * CW, CW), CW)]

    def put(value, c, qi, dst, at, first):
        rows = pl.ds(qi * TILE, TILE)
        value = value - cen[rows, :]
        lanes = pl.ds(pl.multiple_of(c * CW, CW), CW)
        dst[at : at + TILE, lanes] = (value * gains(c)).astype(jnp.bfloat16)
        if first:
            acc[0, rows, :] = value
            acc[1, rows, :] = value * value
        else:
            acc[0, rows, :] += value
            acc[1, rows, :] += value * value

    def attend(c, tiles, dst):
        for qi in tiles:
            n = WINDOW[qi] * TILE
            keys = pl.ds(pl.multiple_of(first_of[qi] * TILE, TILE), n)
            rows = pl.ds(qi * TILE, TILE)
            s = lax.dot_general(
                qb[c, rows, :], kb[c, keys, :], (((1,), (1,)), ((), ())),
                preferred_element_type=jnp.float32,
            )
            s = s + mask[qi, :, :n]
            top = jnp.max(s, axis=-1, keepdims=True)
            p = jnp.exp2((s - top) * SCALE)
            total = jnp.sum(p, axis=-1, keepdims=True)
            o = jnp.dot(
                p.astype(jnp.bfloat16), vb[c, keys, :], preferred_element_type=jnp.float32
            )
            o = o / total
            if dst is None:
                att[c, rows, :] = o
            else:
                put(o, c, qi, dst, (qi - tiles[0]) * TILE, False)

    def center(tiles, dst):
        for qi in tiles:
            rows = pl.ds(qi * TILE, TILE)
            mean = sum(att[c, rows, :] for c in range(HALF))
            mean = jnp.sum(mean, axis=-1, keepdims=True) / (HALF * CW)
            cen[rows, :] = jnp.broadcast_to(mean, (TILE, CW))
            for c in range(HALF):
                put(att[c, rows, :], c, qi, dst, (qi - tiles[0]) * TILE, c == 0)

    def attend_all(tiles, dst, wait):
        def first_half(c, carry):
            wait(c)
            attend(c, tiles, None)
            return carry

        def second_half(c, carry):
            wait(c)
            attend(c, tiles, dst)
            return carry

        lax.fori_loop(0, HALF, first_half, 0)
        center(tiles, dst)
        lax.fori_loop(HALF, NC, second_half, 0)

    def wait_first(c):
        wait_bytes(kb.at[0, 0 : 3 * TILE], q_recv.at[c])
        wait_bytes(kb.at[0, 0 : 6 * TILE], x_recv.at[c])

        @pl.when((c == 2) | (c == 4))
        def _():
            spread_z(1 + c // 2)

    def wait_last(c):
        @pl.when((x == 1) & (c % 2 == 0))
        def _():
            wait_bytes(kb.at[0, 0 : 4 * TILE], l_recv.at[c // 2])

    lane = lax.broadcasted_iota(jnp.int32, (TILE, TILE), 1)

    def statistics(qi):
        rows = pl.ds(qi * TILE, TILE)
        mid = cen[rows, 0:1]
        shift = jnp.sum(acc[0, rows, :], axis=-1, keepdims=True)
        spread = jnp.sum(acc[1, rows, :], axis=-1, keepdims=True) - shift * shift / FEAT
        mean = mid + shift / FEAT
        stat[qi] = jnp.where(lane == 0, mid, jnp.where(lane == 1, mean, spread)).T[:8]

        @pl.when(qi != y)
        def _():
            s_copy(qi).start()

        @pl.when(qi == y)
        def _():
            stat_in[y] = stat[qi]

    for copy in fetch_gains:
        copy.wait()
    wait_bytes(gb.at[:, 0], once_recv.at[1])
    sub = lax.broadcasted_iota(jnp.int32, (EXTRA, CW), 0)
    for c in range(NC):
        half, lanes = c * CW // 512, pl.ds(c * CW % 512, CW)
        value = jnp.zeros((EXTRA, CW), jnp.float32)
        for i in range(2):
            row = gb[i, half, :, lanes]
            high = row.astype(jnp.bfloat16).astype(jnp.float32)
            value = jnp.where(sub == 2 * i, high, jnp.where(sub == 2 * i + 1, row - high, value))
        left[LATE * TILE : ROWS, c * CW : (c + 1) * CW] = value.astype(jnp.bfloat16)

    attend_all(range(LATE), left, wait_first)

    fetch_w.wait()
    wait_bytes(kb, once_recv.at[0])

    def col(half, j):
        return pl.ds(pl.multiple_of(half * 2048 + j * COL, COL), COL)

    def vec_at(i, half, j):
        at = j * COL
        lanes = pl.ds(pl.multiple_of(at % 1024, COL), COL)
        return pl.ds(i * 4 + half * 2 + at // 1024, 1), lanes

    def hand_out(role, half, j, rows, at_once):
        value = pbuf[rows, :]
        if role == 2:
            oppb[half, j] = value.astype(jnp.bfloat16)
            o_copy(half, j).start()
        elif role == 0:
            mixed[half, j] = value
        else:
            way = 0 if role == 1 else 1
            if half == way:
                held[half, j] = value
            else:
                outb[way, half, j] = value.astype(jnp.bfloat16)

                @pl.when(at_once)
                def _():
                    f_copy(way, half, j).start()

    def project(j, carry):
        for half in range(2):
            pbuf[...] = jnp.dot(left[...], wb[:, col(half, j)], preferred_element_type=jnp.float32)
            for role in (2, 1, 3, 0):
                ty = (y + role) % NY

                @pl.when(ty != LATE)
                def _():
                    hand_out(role, half, j, rows_at(ty, TILE), far == LATE)

            extra = pbuf[LATE * TILE : ROWS, :]
            for i in range(2):
                row, lanes = vec_at(i, half, j)
                vec[y, row, lanes] = extra[2 * i : 2 * i + 1] + extra[2 * i + 1 : 2 * i + 2]
        return carry

    lax.fori_loop(0, JC, project, 0)

    def send_direct(j, carry):
        @pl.when((up != LATE) & (far != LATE))
        def _():
            f_copy(0, 1, j).start()

        @pl.when((down != LATE) & (far != LATE))
        def _():
            f_copy(1, 0, j).start()

        return carry

    lax.fori_loop(0, JC, send_direct, 0)
    for n in (1, 3, 2):
        v_copy(n).start()
    for qi in range(LATE):
        statistics(qi)

    def pass_on(half, j):
        wait_bytes(rel.at[half, j], o_recv.at[half, j])
        value = held[half, j] + rel[half, j].astype(jnp.float32)
        outb[half, half, j] = value.astype(jnp.bfloat16)
        f_copy(half, half, j).start()

    def pass_first(j, carry):
        for half in range(2):

            @pl.when((up, down)[half] != LATE)
            def _():
                pass_on(half, j)

        return carry

    lax.fori_loop(0, JC // 2, pass_first, 0)

    attend_all((LATE,), left_late, wait_last)

    def project_late(j, carry):
        for half in range(2):
            pbuf[:TILE] = jnp.dot(
                left_late[...], wb[:, col(half, j)], preferred_element_type=jnp.float32
            )
            for role in (2, 1, 3, 0):

                @pl.when((y + role) % NY == LATE)
                def _():
                    hand_out(role, half, j, pl.ds(0, TILE), y >= 0)

        return carry

    lax.fori_loop(0, JC, project_late, 0)

    statistics(LATE)
    wait_bytes(wb.at[0:288], sent_sem.at[0])
    wait_bytes(kb.at[0:6], sent_sem.at[1])

    @pl.when(x == 0)
    def _():
        wait_bytes(kb.at[0:2], sent_sem.at[2])

    wait_bytes(wb.at[0:512], sent_sem.at[3])
    wait_bytes(gb.at[:, 0], sent_sem.at[4])
    wait_bytes(stat.at[0:3], sent_sem.at[5])
    wait_bytes(vec.at[0:3], sent_sem.at[6])

    def pass_late(j, carry):
        for half in range(2):

            @pl.when((up, down)[half] == LATE)
            def _():
                pass_on(half, j)

        return carry

    lax.fori_loop(JC // 2, JC, pass_first, 0)
    lax.fori_loop(0, JC, pass_late, 0)

    wait_bytes(stat_in.at[0:3], once_recv.at[2])
    wait_bytes(vec.at[0:3], once_recv.at[3])
    for copy in fetch_rest:
        copy.wait()

    means = [stat_in[ty, 1:2, :] for ty in range(NY)]
    mean = sum(means) / NY
    spread = sum(stat_in[ty, 2:3, :] for ty in range(NY))
    spread = spread + FEAT * sum((m - mean) ** 2 for m in means)
    inv = lax.rsqrt(spread / (NY * FEAT) + 1e-05)
    sub = lax.broadcasted_iota(jnp.int32, (TILE, TILE), 0)
    both = jnp.broadcast_to(inv, (TILE, TILE))
    for ty in range(NY):
        both = jnp.where(sub == ty, stat_in[ty, 0:1, :] - mean, both)
    both = both.T
    inv = both[:, NY : NY + 1]

    def prepare(j, carry):
        for half in range(2):
            value = mixed[half, j]
            shift = jnp.zeros((1, COL), jnp.float32)
            for ty in range(NY):
                row, lanes = vec_at(0, half, j)
                value = value + both[:, ty : ty + 1] * vec[ty, row, lanes]
                row, lanes = vec_at(1, half, j)
                shift = shift + vec[ty, row, lanes]
            stream = deep_alpha * resb[:, col(half, j)].astype(jnp.float32)
            mixed[half, j] = value * inv + shift + stream
        return carry

    lax.fori_loop(0, JC, prepare, 0)

    def m_copy(half, j):
        return pltpu.make_async_copy(
            final.at[half, j], out.at[:, col(half, j)], loc_sem.at[7]
        )

    def arrive(half, j):
        wait_bytes(fin.at[:, half, j], f_recv.at[half, j])
        value = fin[0, half, j].astype(jnp.float32) + fin[1, half, j].astype(jnp.float32)
        value = mixed[half, j] + inv * value
        mixed[half, j] = value
        return value

    start = [arrive(half, 0) for half in range(2)]
    mid = sum(jnp.sum(value, axis=-1, keepdims=True) for value in start) / (2 * COL)
    spread = sum(jnp.sum((value - mid) ** 2, axis=-1, keepdims=True) for value in start)

    def collect(j, carry):
        total, spread = carry
        for half in range(2):
            value = arrive(half, j) - mid
            total = total + jnp.sum(value, axis=-1, keepdims=True)
            spread = spread + jnp.sum(value * value, axis=-1, keepdims=True)
        return total, spread

    total, spread = lax.fori_loop(1, JC, collect, (jnp.zeros((TILE, 1), jnp.float32), spread))
    mean = mid + total / D
    spread = spread - total * total / D
    inv = lax.rsqrt(spread / D + 1e-05)
    for half in range(2):
        for j in range(JC):
            lanes = pl.ds(half * 2048 + j * COL, COL)
            value = (mixed[half, j] - mean) * inv * pgb[:, lanes] + pbb[:, lanes]
            final[half, j] = value.astype(jnp.bfloat16)
            m_copy(half, j).start()
    wait_bytes(final, loc_sem.at[7])
    wait_bytes(oppb, sent_sem.at[7])
    wait_bytes(outb, sent_sem.at[8])


def body(
    queries, keys, values, segment_ids, residual, sub_gain, sub_bias, out_weight, post_gain, post_bias
):
    any_spec = pl.BlockSpec(memory_space=pl.ANY)
    bf16, f32 = jnp.bfloat16, jnp.float32
    dma = pltpu.SemaphoreType.DMA
    return pl.pallas_call(
        kernel,
        name="block",
        out_shape=jax.ShapeDtypeStruct((TILE, D), bf16),
        in_specs=[any_spec] * 10,
        out_specs=any_spec,
        scratch_shapes=[
            pltpu.VMEM((TILE, D), bf16),
            pltpu.VMEM((TILE, D), bf16),
            pltpu.VMEM((TILE, D), bf16),
            pltpu.VMEM((NC, NY * TILE, CW), bf16),
            pltpu.VMEM((NC, 8 * TILE, CW), bf16),
            pltpu.VMEM((NC, 8 * TILE, CW), bf16),
            pltpu.VMEM((FEAT, D), bf16),
            pltpu.VMEM((2, 2, 1, 512), f32),
            pltpu.VMEM((NY, TILE, 5 * TILE), f32),
            pltpu.VMEM((HALF, NY * TILE, CW), f32),
            pltpu.VMEM((NY * TILE, CW), f32),
            pltpu.VMEM((2, NY * TILE, CW), f32),
            pltpu.VMEM((ROWS, FEAT), bf16),
            pltpu.VMEM((TILE, FEAT), bf16),
            pltpu.VMEM((NY, 8, TILE), f32),
            pltpu.VMEM((NY, 8, TILE), f32),
            pltpu.VMEM((NY, 8, D // 4), f32),
            pltpu.VMEM((ROWS, COL), f32),
            pltpu.VMEM((2, JC, TILE, COL), bf16),
            pltpu.VMEM((2, JC, TILE, COL), bf16),
            pltpu.VMEM((2, JC, TILE, COL), f32),
            pltpu.VMEM((2, 2, JC, TILE, COL), bf16),
            pltpu.VMEM((2, 2, JC, TILE, COL), bf16),
            pltpu.VMEM((2, JC, TILE, COL), f32),
            pltpu.VMEM((2, JC, TILE, COL), bf16),
            pltpu.VMEM((TILE, D), bf16),
            pltpu.VMEM((1, D), f32),
            pltpu.VMEM((1, D), f32),
            pltpu.VMEM((8, TILE), jnp.int32),
            dma((11,)),
            dma((9,)),
            dma((NC,)),
            dma((NC,)),
            dma((NC,)),
            dma((NC // 2,)),
            dma((WN,)),
            dma((WN,)),
            dma((2, JC)),
            dma((2, JC)),
            dma((4,)),
        ],
        compiler_params=pltpu.CompilerParams(
            collective_id=0, has_side_effects=True, vmem_limit_bytes=56 << 20
        ),
    )(
        queries,
        keys,
        values,
        segment_ids.reshape(8, TILE),
        residual,
        sub_gain.reshape(1, 512),
        sub_bias.reshape(1, 512),
        out_weight,
        post_gain.reshape(1, D),
        post_bias.reshape(1, D),
    )


def solution(mesh):
    return jax.shard_map(
        body,
        mesh=mesh,
        in_specs=(
            P(("dp", "tensor"), None),
            P(("dp", "tensor"), None),
            P(("dp", "tensor"), None),
            P("dp"),
            P(("dp", "tensor"), None),
            P("tensor"),
            P("tensor"),
            P("tensor", None),
            P(),
            P(),
        ),
        out_specs=P(("dp", "tensor"), None),
        check_vma=False,
    )
```

```python
import jax
import jax.numpy as jnp
from jax import lax
from jax.experimental import pallas as pl
from jax.experimental.pallas import tpu as pltpu
from jax.sharding import PartitionSpec as P

HEAD_DIM = 128
TILE = 128
D = 4096
NY = 4
LATE = NY - 1
FEAT = 1024
NC = 8
CW = FEAT // NC
HALF = NC // 2
EARLY = 3 * NC // 8
WN = 4
WROWS = 128 // WN
JC = 4
COL = 2048 // JC
EXTRA = 16
ROWS = LATE * TILE + EXTRA
WINDOW = (2, 4, 5, 5)
MESH = pl.DeviceIdType.MESH

deep_alpha = 160.0**0.25
LOG2E = 1.4426950408889634
SCALE = LOG2E / HEAD_DIM**0.5


def kernel(
    q, k, v, seg_in, res, gain, bias, w, pg, pb,
    out,
    qs, ks, vs, qb, kb, vb, wb, gb, mask, att, cen, acc, left, left_late, stat, stat_in, vec, pbuf,
    oppb, rel, held, outb, fin, mixed, final, resb, pgb, pbb, seg,
    loc_sem, sent_sem, kv_recv, q_recv, x_recv, l_recv, w_recv, z_recv, o_recv, f_recv, once_recv,
):
    dp = lax.axis_index("dp")
    t = lax.axis_index("tensor")
    core, hi, z = dp % 2, (dp // 2) % 2, dp // 4
    x, y = t % 2, t // 2
    zpar = z % 2

    def y_dev(ty):
        return {"dp": dp, "tensor": ty * 2 + x}

    x_dev = {"dp": dp, "tensor": y * 2 + (1 - x)}
    wrap_dev = {"dp": z * 4 + (1 - hi) * 2 + core, "tensor": y * 2 + (1 - x)}
    core_dev = {"dp": z * 4 + hi * 2 + (1 - core), "tensor": t}
    z_dev = {"dp": (z + 1 - 2 * zpar) * 4 + hi * 2 + core, "tensor": t}
    up, far, down = (y + 1) % NY, (y + 2) % NY, (y + 3) % NY

    def remote(src, dst, ss, rs, dev):
        return pltpu.make_async_remote_copy(
            src_ref=src, dst_ref=dst, send_sem=ss, recv_sem=rs, device_id=dev, device_id_type=MESH
        )

    def wait_bytes(ref, sem):
        pltpu.make_async_copy(ref, ref, sem).wait()

    def rows_at(n, size):
        return pl.ds(pl.multiple_of(n * size, size), size)

    def cols(ty, c):
        return pl.ds(pl.multiple_of(ty * FEAT + c * CW, CW), CW)

    def slot(a, ty, c):
        if a == 0:
            return qb.at[c, rows_at(ty, TILE)]
        return (kb, vb)[a - 1].at[c, rows_at(2 * ty + x, TILE)]

    def y_copy(n, c, a):
        ty = (y + n) % NY
        sem = q_recv if a == 0 else kv_recv
        return remote(
            (qs, ks, vs)[a].at[:, cols(ty, c)], slot(a, y, c), sent_sem.at[0], sem.at[c], y_dev(ty)
        )

    def x_copy(ty, c, a):
        dst = slot(a, ty, c)
        return remote(dst, dst, sent_sem.at[1], x_recv.at[c], x_dev)

    def x_own(c, a):
        return remote(
            (qs, ks, vs)[a].at[:, cols(y, c)], slot(a, y, c), sent_sem.at[1], x_recv.at[c], x_dev
        )

    def l_copy(c, a):
        dst = slot(a, LATE, c)
        return remote(dst, dst, sent_sem.at[2], l_recv.at[c // 2], x_dev)

    def l_own(c, a):
        return remote(
            (qs, ks, vs)[a].at[:, cols(y, c)], slot(a, y, c), sent_sem.at[2], l_recv.at[c // 2], x_dev
        )

    def piece(owner, of_core, of_z, n):
        return wb.at[rows_at(owner * 16 + of_core * 8 + of_z * 4 + n, WROWS)]

    def w_copy(n):
        src = w.at[rows_at(core * 8 + zpar * 4 + n, WROWS)]
        return remote(src, piece(x, core, zpar, n), sent_sem.at[3], w_recv.at[n], wrap_dev)

    def w_wait(n):
        wait_bytes(piece(1 - x, core, zpar, n), w_recv.at[n])

    def z_copy(n):
        src = piece(1 - x, core, zpar, n)
        return remote(src, src, sent_sem.at[3], z_recv.at[n], z_dev)

    def z_wait(n):
        wait_bytes(piece(1 - x, core, 1 - zpar, n), z_recv.at[n])

    def c_copy(of_z, n):
        src = piece(1 - x, core, of_z, n)
        return remote(src, src, sent_sem.at[3], once_recv.at[0], core_dev)

    def g_copy(i):
        return remote((gain, bias)[i], gb.at[i, x], sent_sem.at[4], once_recv.at[1], wrap_dev)

    def s_copy(ty):
        return remote(stat.at[ty], stat_in.at[y], sent_sem.at[5], once_recv.at[2], y_dev(ty))

    def v_copy(n):
        return remote(vec.at[y], vec.at[y], sent_sem.at[6], once_recv.at[3], y_dev((y + n) % NY))

    def o_copy(half, j):
        return remote(
            oppb.at[half, j], rel.at[half, j], sent_sem.at[7], o_recv.at[half, j],
            y_dev((up, down)[half]),
        )

    def f_copy(way, half, j):
        return remote(
            outb.at[way, half, j], fin.at[way, half, j], sent_sem.at[8],
            f_recv.at[half, j], y_dev((up, down)[way]),
        )

    def fetch(src, dst, n):
        return pltpu.make_async_copy(src, dst, loc_sem.at[n])

    stage = [fetch((q, k, v)[a], (qs, ks, vs)[a], 8 + a) for a in range(3)]
    for a in (1, 2, 0):
        stage[a].start()
    fetch_seg = fetch(seg_in, seg, 0)
    fetch_seg.start()

    barrier = pltpu.get_barrier_semaphore()
    peers = [y_dev(up), y_dev(far), y_dev(down), x_dev, wrap_dev, core_dev, z_dev]
    for dev in peers:
        pl.semaphore_signal(barrier, inc=1, device_id=dev, device_id_type=MESH)
    pl.semaphore_wait(barrier, len(peers))

    def send_kv(c, carry):
        for a in (1, 2):
            for n in (1, 3, 2):
                y_copy(n, c, a).start()

        @pl.when(y != LATE)
        def _():
            for a in (1, 2):
                x_own(c, a).start()

        @pl.when((y == LATE) & (x == 0) & (c < EARLY))
        def _():
            for a in (1, 2):
                l_own(c, a).start()

        return carry

    def send_q(c, carry):
        for n in (1, 3, 2):
            y_copy(n, c, 0).start()
        return carry

    stage[1].wait()
    stage[2].wait()
    lax.fori_loop(0, 1, send_kv, 0)
    for n in range(WN):
        w_copy(n).start()
    lax.fori_loop(1, NC, send_kv, 0)
    for i in range(2):
        g_copy(i).start()
    stage[0].wait()
    lax.fori_loop(0, NC, send_q, 0)

    def fetch_own(c, carry):
        for a in range(3):
            fetch((qs, ks, vs)[a].at[:, cols(y, c)], slot(a, y, c), 1).start()
        return carry

    lax.fori_loop(0, NC, fetch_own, 0)
    fetch_gains = [fetch(gain, gb.at[0, x], 2), fetch(bias, gb.at[1, x], 2)]
    fetch_w = fetch(w, wb.at[rows_at(x, 512)], 3)
    fetch_rest = [fetch(pg, pgb, 4), fetch(pb, pbb, 5), fetch(res, resb, 6)]
    for copy in fetch_gains + [fetch_w] + fetch_rest:
        copy.start()

    fetch_seg.wait()

    first_of = (0, 0, x, 2 + x)
    for qi in range(NY):
        tq = 2 * qi + x
        row = seg[pl.ds(tq, 1), :].astype(jnp.float32)
        of_query = jnp.broadcast_to(row, (TILE, TILE)).T
        sub = lax.broadcasted_iota(jnp.int32, (TILE, TILE), 0) + tq * TILE
        lane = lax.broadcasted_iota(jnp.int32, (TILE, TILE), 1)
        for n in range(WINDOW[qi]):
            of_key = seg[pl.ds(first_of[qi] + n, 1), :].astype(jnp.float32)
            seen = (of_query == of_key) & (lane + (first_of[qi] + n) * TILE <= sub)
            mask[qi, :, n * TILE : (n + 1) * TILE] = jnp.where(seen, 0.0, -1e30)

    wait_bytes(kb.at[0:3], loc_sem.at[1])

    def receive_kv(c):
        wait_bytes(kb.at[0, 0 : 6 * TILE], kv_recv.at[c])
        for ty in range(LATE):

            @pl.when(ty != y)
            def _():
                for a in (1, 2):
                    x_copy(ty, c, a).start()

    def spread_z(n):
        z_wait(n)
        c_copy(1 - zpar, n).start()

    def relay(i, carry):
        for h in range(NC // WN):
            receive_kv(i * (NC // WN) + h)
        w_wait(i)
        c_copy(zpar, i).start()
        z_copy(i).start()

        @pl.when(i >= 2)
        def _():
            spread_z(i - 2)

        return carry

    lax.fori_loop(0, WN, relay, 0)

    def relay_late(c, carry):
        @pl.when((x == 0) & ((y != LATE) | (c >= EARLY)))
        def _():
            for a in (1, 2):
                l_copy(c, a).start()

        return carry

    lax.fori_loop(0, NC, relay_late, 0)

    def gains(c):
        return gb[0, c // 4, :, pl.ds(pl.multiple_of((c % 4) * CW, CW), CW)]

    def put(value, c, qi, dst, at, first):
        rows = pl.ds(qi * TILE, TILE)
        value = value - cen[rows, :]
        lanes = pl.ds(pl.multiple_of(c * CW, CW), CW)
        dst[at : at + TILE, lanes] = (value * gains(c)).astype(jnp.bfloat16)
        if first:
            acc[0, rows, :] = value
            acc[1, rows, :] = value * value
        else:
            acc[0, rows, :] += value
            acc[1, rows, :] += value * value

    def attend(c, tiles, dst):
        for qi in tiles:
            n = WINDOW[qi] * TILE
            keys = pl.ds(pl.multiple_of(first_of[qi] * TILE, TILE), n)
            rows = pl.ds(qi * TILE, TILE)
            s = lax.dot_general(
                qb[c, rows, :], kb[c, keys, :], (((1,), (1,)), ((), ())),
                preferred_element_type=jnp.float32,
            )
            s = s + mask[qi, :, :n]
            top = jnp.max(s, axis=-1, keepdims=True)
            p = jnp.exp2((s - top) * SCALE)
            total = jnp.sum(p, axis=-1, keepdims=True)
            o = jnp.dot(
                p.astype(jnp.bfloat16), vb[c, keys, :], preferred_element_type=jnp.float32
            )
            o = o / total
            if dst is None:
                att[c, rows, :] = o
            else:
                put(o, c, qi, dst, (qi - tiles[0]) * TILE, False)

    def center(tiles, dst):
        for qi in tiles:
            rows = pl.ds(qi * TILE, TILE)
            mean = sum(att[c, rows, :] for c in range(HALF))
            mean = jnp.sum(mean, axis=-1, keepdims=True) / (HALF * CW)
            cen[rows, :] = jnp.broadcast_to(mean, (TILE, CW))
            for c in range(HALF):
                put(att[c, rows, :], c, qi, dst, (qi - tiles[0]) * TILE, c == 0)

    def attend_all(tiles, dst, wait):
        def first_half(c, carry):
            wait(c)
            attend(c, tiles, None)
            return carry

        def second_half(c, carry):
            wait(c)
            attend(c, tiles, dst)
            return carry

        lax.fori_loop(0, HALF, first_half, 0)
        center(tiles, dst)
        lax.fori_loop(HALF, NC, second_half, 0)

    def wait_first(c):
        wait_bytes(kb.at[0, 0 : 3 * TILE], q_recv.at[c])
        wait_bytes(kb.at[0, 0 : 6 * TILE], x_recv.at[c])

        @pl.when((c == 2) | (c == 4))
        def _():
            spread_z(1 + c // 2)

    def wait_last(c):
        @pl.when((x == 1) & (c % 2 == 0))
        def _():
            wait_bytes(kb.at[0, 0 : 4 * TILE], l_recv.at[c // 2])

    lane = lax.broadcasted_iota(jnp.int32, (TILE, TILE), 1)

    def statistics(qi):
        rows = pl.ds(qi * TILE, TILE)
        mid = cen[rows, 0:1]
        shift = jnp.sum(acc[0, rows, :], axis=-1, keepdims=True)
        spread = jnp.sum(acc[1, rows, :], axis=-1, keepdims=True) - shift * shift / FEAT
        mean = mid + shift / FEAT
        stat[qi] = jnp.where(lane == 0, mid, jnp.where(lane == 1, mean, spread)).T[:8]

        @pl.when(qi != y)
        def _():
            s_copy(qi).start()

        @pl.when(qi == y)
        def _():
            stat_in[y] = stat[qi]

    for copy in fetch_gains:
        copy.wait()
    wait_bytes(gb.at[:, 0], once_recv.at[1])
    sub = lax.broadcasted_iota(jnp.int32, (EXTRA, CW), 0)
    for c in range(NC):
        half, lanes = c * CW // 512, pl.ds(c * CW % 512, CW)
        value = jnp.zeros((EXTRA, CW), jnp.float32)
        for i in range(2):
            row = gb[i, half, :, lanes]
            high = row.astype(jnp.bfloat16).astype(jnp.float32)
            value = jnp.where(sub == 2 * i, high, jnp.where(sub == 2 * i + 1, row - high, value))
        left[LATE * TILE : ROWS, c * CW : (c + 1) * CW] = value.astype(jnp.bfloat16)

    attend_all(range(LATE), left, wait_first)

    fetch_w.wait()
    wait_bytes(kb, once_recv.at[0])

    def col(half, j):
        return pl.ds(pl.multiple_of(half * 2048 + j * COL, COL), COL)

    def vec_at(i, half, j):
        at = j * COL
        lanes = pl.ds(pl.multiple_of(at % 1024, COL), COL)
        return pl.ds(i * 4 + half * 2 + at // 1024, 1), lanes

    def hand_out(role, half, j, rows, at_once):
        value = pbuf[rows, :]
        if role == 2:
            oppb[half, j] = value.astype(jnp.bfloat16)
            o_copy(half, j).start()
        elif role == 0:
            mixed[half, j] = value
        else:
            way = 0 if role == 1 else 1
            if half == way:
                held[half, j] = value
            else:
                outb[way, half, j] = value.astype(jnp.bfloat16)

                @pl.when(at_once)
                def _():
                    f_copy(way, half, j).start()

    def project(j, carry):
        for half in range(2):
            pbuf[...] = jnp.dot(left[...], wb[:, col(half, j)], preferred_element_type=jnp.float32)
            for role in (2, 1, 3, 0):
                ty = (y + role) % NY

                @pl.when(ty != LATE)
                def _():
                    hand_out(role, half, j, rows_at(ty, TILE), far == LATE)

            extra = pbuf[LATE * TILE : ROWS, :]
            for i in range(2):
                row, lanes = vec_at(i, half, j)
                vec[y, row, lanes] = extra[2 * i : 2 * i + 1] + extra[2 * i + 1 : 2 * i + 2]
        return carry

    lax.fori_loop(0, JC, project, 0)

    def send_direct(j, carry):
        @pl.when((up != LATE) & (far != LATE))
        def _():
            f_copy(0, 1, j).start()

        @pl.when((down != LATE) & (far != LATE))
        def _():
            f_copy(1, 0, j).start()

        return carry

    lax.fori_loop(0, JC, send_direct, 0)
    for n in (1, 3, 2):
        v_copy(n).start()
    for qi in range(LATE):
        statistics(qi)

    def pass_on(half, j):
        wait_bytes(rel.at[half, j], o_recv.at[half, j])
        value = held[half, j] + rel[half, j].astype(jnp.float32)
        outb[half, half, j] = value.astype(jnp.bfloat16)
        f_copy(half, half, j).start()

    def pass_first(j, carry):
        for half in range(2):

            @pl.when((up, down)[half] != LATE)
            def _():
                pass_on(half, j)

        return carry

    lax.fori_loop(0, JC // 2, pass_first, 0)

    attend_all((LATE,), left_late, wait_last)

    def project_late(j, carry):
        for half in range(2):
            pbuf[:TILE] = jnp.dot(
                left_late[...], wb[:, col(half, j)], preferred_element_type=jnp.float32
            )
            for role in (2, 1, 3, 0):

                @pl.when((y + role) % NY == LATE)
                def _():
                    hand_out(role, half, j, pl.ds(0, TILE), y >= 0)

        return carry

    lax.fori_loop(0, JC, project_late, 0)

    statistics(LATE)
    wait_bytes(wb.at[0:288], sent_sem.at[0])
    wait_bytes(kb.at[0:6], sent_sem.at[1])

    @pl.when(x == 0)
    def _():
        wait_bytes(kb.at[0:2], sent_sem.at[2])

    wait_bytes(wb.at[0:512], sent_sem.at[3])
    wait_bytes(gb.at[:, 0], sent_sem.at[4])

    def pass_late(j, carry):
        for half in range(2):

            @pl.when((up, down)[half] == LATE)
            def _():
                pass_on(half, j)

        return carry

    lax.fori_loop(JC // 2, JC, pass_first, 0)
    lax.fori_loop(0, JC, pass_late, 0)

    wait_bytes(stat_in.at[0:3], once_recv.at[2])
    wait_bytes(vec.at[0:3], once_recv.at[3])
    for copy in fetch_rest:
        copy.wait()

    means = [stat_in[ty, 1:2, :] for ty in range(NY)]
    mean = sum(means) / NY
    spread = sum(stat_in[ty, 2:3, :] for ty in range(NY))
    spread = spread + FEAT * sum((m - mean) ** 2 for m in means)
    inv = lax.rsqrt(spread / (NY * FEAT) + 1e-05)
    sub = lax.broadcasted_iota(jnp.int32, (TILE, TILE), 0)
    both = jnp.broadcast_to(inv, (TILE, TILE))
    for ty in range(NY):
        both = jnp.where(sub == ty, stat_in[ty, 0:1, :] - mean, both)
    both = both.T
    inv = both[:, NY : NY + 1]

    def prepare(j, carry):
        for half in range(2):
            value = mixed[half, j]
            shift = jnp.zeros((1, COL), jnp.float32)
            for ty in range(NY):
                row, lanes = vec_at(0, half, j)
                value = value + both[:, ty : ty + 1] * vec[ty, row, lanes]
                row, lanes = vec_at(1, half, j)
                shift = shift + vec[ty, row, lanes]
            stream = deep_alpha * resb[:, col(half, j)].astype(jnp.float32)
            mixed[half, j] = value * inv + shift + stream
        return carry

    lax.fori_loop(0, JC, prepare, 0)

    def m_copy(half, j):
        return pltpu.make_async_copy(
            final.at[half, j], out.at[:, col(half, j)], loc_sem.at[7]
        )

    def arrive(half, j):
        wait_bytes(fin.at[:, half, j], f_recv.at[half, j])
        value = fin[0, half, j].astype(jnp.float32) + fin[1, half, j].astype(jnp.float32)
        value = mixed[half, j] + inv * value
        mixed[half, j] = value
        return value

    start = [arrive(half, 0) for half in range(2)]
    mid = sum(jnp.sum(value, axis=-1, keepdims=True) for value in start) / (2 * COL)
    spread = sum(jnp.sum((value - mid) ** 2, axis=-1, keepdims=True) for value in start)

    def collect(j, carry):
        total, spread = carry
        for half in range(2):
            value = arrive(half, j) - mid
            total = total + jnp.sum(value, axis=-1, keepdims=True)
            spread = spread + jnp.sum(value * value, axis=-1, keepdims=True)
        return total, spread

    total, spread = lax.fori_loop(1, JC, collect, (jnp.zeros((TILE, 1), jnp.float32), spread))
    mean = mid + total / D
    spread = spread - total * total / D
    inv = lax.rsqrt(spread / D + 1e-05)
    for half in range(2):
        for j in range(JC):
            lanes = pl.ds(half * 2048 + j * COL, COL)
            value = (mixed[half, j] - mean) * inv * pgb[:, lanes] + pbb[:, lanes]
            final[half, j] = value.astype(jnp.bfloat16)
            m_copy(half, j).start()
    wait_bytes(final, loc_sem.at[7])
    wait_bytes(stat.at[0:3], sent_sem.at[5])
    wait_bytes(vec.at[0:3], sent_sem.at[6])
    wait_bytes(oppb, sent_sem.at[7])
    wait_bytes(outb, sent_sem.at[8])


def body(
    queries, keys, values, segment_ids, residual, sub_gain, sub_bias, out_weight, post_gain, post_bias
):
    any_spec = pl.BlockSpec(memory_space=pl.ANY)
    bf16, f32 = jnp.bfloat16, jnp.float32
    dma = pltpu.SemaphoreType.DMA
    return pl.pallas_call(
        kernel,
        name="block",
        out_shape=jax.ShapeDtypeStruct((TILE, D), bf16),
        in_specs=[any_spec] * 10,
        out_specs=any_spec,
        scratch_shapes=[
            pltpu.VMEM((TILE, D), bf16),
            pltpu.VMEM((TILE, D), bf16),
            pltpu.VMEM((TILE, D), bf16),
            pltpu.VMEM((NC, NY * TILE, CW), bf16),
            pltpu.VMEM((NC, 8 * TILE, CW), bf16),
            pltpu.VMEM((NC, 8 * TILE, CW), bf16),
            pltpu.VMEM((FEAT, D), bf16),
            pltpu.VMEM((2, 2, 1, 512), f32),
            pltpu.VMEM((NY, TILE, 5 * TILE), f32),
            pltpu.VMEM((HALF, NY * TILE, CW), f32),
            pltpu.VMEM((NY * TILE, CW), f32),
            pltpu.VMEM((2, NY * TILE, CW), f32),
            pltpu.VMEM((ROWS, FEAT), bf16),
            pltpu.VMEM((TILE, FEAT), bf16),
            pltpu.VMEM((NY, 8, TILE), f32),
            pltpu.VMEM((NY, 8, TILE), f32),
            pltpu.VMEM((NY, 8, D // 4), f32),
            pltpu.VMEM((ROWS, COL), f32),
            pltpu.VMEM((2, JC, TILE, COL), bf16),
            pltpu.VMEM((2, JC, TILE, COL), bf16),
            pltpu.VMEM((2, JC, TILE, COL), f32),
            pltpu.VMEM((2, 2, JC, TILE, COL), bf16),
            pltpu.VMEM((2, 2, JC, TILE, COL), bf16),
            pltpu.VMEM((2, JC, TILE, COL), f32),
            pltpu.VMEM((2, JC, TILE, COL), bf16),
            pltpu.VMEM((TILE, D), bf16),
            pltpu.VMEM((1, D), f32),
            pltpu.VMEM((1, D), f32),
            pltpu.VMEM((8, TILE), jnp.int32),
            dma((11,)),
            dma((9,)),
            dma((NC,)),
            dma((NC,)),
            dma((NC,)),
            dma((NC // 2,)),
            dma((WN,)),
            dma((WN,)),
            dma((2, JC)),
            dma((2, JC)),
            dma((4,)),
        ],
        compiler_params=pltpu.CompilerParams(
            collective_id=0, has_side_effects=True, vmem_limit_bytes=56 << 20
        ),
    )(
        queries,
        keys,
        values,
        segment_ids.reshape(8, TILE),
        residual,
        sub_gain.reshape(1, 512),
        sub_bias.reshape(1, 512),
        out_weight,
        post_gain.reshape(1, D),
        post_bias.reshape(1, D),
    )


def solution(mesh):
    return jax.shard_map(
        body,
        mesh=mesh,
        in_specs=(
            P(("dp", "tensor"), None),
            P(("dp", "tensor"), None),
            P(("dp", "tensor"), None),
            P("dp"),
            P(("dp", "tensor"), None),
            P("tensor"),
            P("tensor"),
            P("tensor", None),
            P(),
            P(),
        ),
        out_specs=P(("dp", "tensor"), None),
        check_vma=False,
    )
```
